32 devices in a mesh: seq: 4 (over z), head: 8 (over y, x, core).
Axes of the slice: x: 2, y: 2, z: 4, core: 2. Of those that a mesh axis runs over, the one named last changes fastest.
Arguments:
- tokens: bfloat16 [4096, 4096], P(('seq', 'head')), may hold values from -6 to 6
- doc_lengths: int32 [16], replicated, may hold values from 1 to 2560, as said below
- value_weight: bfloat16 [4096, 8192], P('seq', 'head'), may hold values from -0.09375 to 0.09375
- gate_weight: bfloat16 [4096, 8192], P('seq', 'head'), may hold values from -0.09375 to 0.09375
- state_weight: bfloat16 [8, 4096, 256], P(None, 'seq'), may hold values from -0.09375 to 0.09375
- step_weight: bfloat16 [4096, 128], P('seq', 'head'), may hold values from -0.09375 to 0.09375
- value_conv: float32 [4, 8192], P(None, 'head'), may hold values from -3 to 3
- state_conv: float32 [8, 4, 256], replicated, may hold values from -3 to 3
- step_bias: float32 [128], P('head'), may hold values from -5 to -3
- log_rate: float32 [128], P('head'), may hold values from -6 to 4
Outputs:
- layer_output: bfloat16 [4096, 8192], P('seq', 'head')
The draws below stay inside these ranges and needn't reach their ends.
Inputs may be any that keep to these rules, and one draw needn't show every extreme that they name: `doc_lengths`: the 16 documents lie one after another, their lengths sum to 4096, and the last one holds 2560 positions.
All inputs are finite; a program needn't handle non-finite values.
Results may differ from the reference program's by a relative error of at most 0.015.
Values may be sent and summed in bfloat16 or wider, within the bound.
A program may use at most 128 MiB of HBM per device.

```python
import jax
import jax.numpy as jnp
from jax import lax

D = 4096
HEADS = 128
HEAD_DIM = 64
STATE = 128
GROUPS = 8
BLOCK = 256
CONV = 4
DOCS = 16
TOK_DEV = 1024
TOKENS = 4096


def draw_doc_lengths(key, part):
    longest = TOKENS // 2 + TOK_DEV // 2
    remaining = TOKENS - longest
    shuffled = jax.random.permutation(jax.random.fold_in(key, 17), remaining - 1)
    cut_points = jnp.sort(shuffled[:DOCS - 2] + 1).astype(jnp.int32)
    edges = jnp.concatenate([jnp.zeros((1,), jnp.int32), cut_points, jnp.full((1,), remaining, jnp.int32)])
    leading = (edges[1:] - edges[:-1]).astype(jnp.int32)
    return jnp.concatenate([leading, jnp.full((1,), longest, jnp.int32)]).astype(jnp.int32)


def block_levels(stream_key, shape, split, low, high):
    factor_of, own = 1.0, jax.random.fold_in(stream_key, 6)
    for dim, parts in split:
        steps = jnp.exp(jax.random.uniform(jax.random.fold_in(own, dim), (parts,), jnp.float32, low / len(split), high / len(split)))
        factor_of = factor_of * jnp.repeat(steps, shape[dim] // parts).reshape([-1 if axis == dim else 1 for axis in range(len(shape))])
    return factor_of


def noise(key, dims, scale, bound, cuts=(), held_as=jnp.bfloat16):
    array = scale * jax.random.normal(key, dims, jnp.float32)
    if cuts:
        array = array * block_levels(key, dims, cuts, -0.22, 0.18)
    return jnp.clip(array, -bound, bound).astype(held_as)


def setup_inputs(seed: int = 0) -> dict:
    splits = jax.random.split(jax.random.key(seed), 11)
    tokens = noise(splits[0], (TOKENS, D), 1.0, 6.0, ((0, 32),))
    doc_lengths = draw_doc_lengths(jax.random.fold_in(splits[10], 71), 0)
    value_weight = noise(splits[2], (D, HEADS * HEAD_DIM), D ** -0.5, 0.09375, ((0, 4), (1, 8)))
    gate_weight = noise(splits[3], (D, HEADS * HEAD_DIM), D ** -0.5, 0.09375, ((0, 4), (1, 8)))
    state_weight = noise(splits[4], (GROUPS, D, 2 * STATE), D ** -0.5, 0.09375, ((1, 4),))
    step_weight = noise(splits[5], (D, HEADS), D ** -0.5, 0.09375, ((0, 4), (1, 8)))
    value_conv = noise(splits[6], (CONV, HEADS * HEAD_DIM), CONV ** -0.5, 3.0, ((1, 8),), jnp.float32)
    state_conv = noise(splits[7], (GROUPS, CONV, 2 * STATE), CONV ** -0.5, 3.0, (), jnp.float32)
    step_bias = jnp.clip(-5.0 + 2.0 * jax.random.uniform(splits[8], (HEADS,), jnp.float32) ** block_levels(splits[8], (HEADS,), ((0, 8),), -0.2, 0.2), -5.0, -3.0)
    log_rate = jnp.clip(-6.0 + 10.0 * jax.random.uniform(splits[9], (HEADS,), jnp.float32) ** block_levels(splits[9], (HEADS,), ((0, 8),), -0.2, 0.2), -6.0, 4.0)
    return {"tokens": tokens, "doc_lengths": doc_lengths, "value_weight": value_weight, "gate_weight": gate_weight, "state_weight": state_weight, "step_weight": step_weight, "value_conv": value_conv, "state_conv": state_conv, "step_bias": step_bias, "log_rate": log_rate}


def segment_of(positions, starts):
    reached = (starts[None, :] <= positions[:, None]).astype(jnp.int32)
    return (jnp.sum(reached, axis=1) - 1).astype(jnp.int32)


def causal_conv(extended, taps_weight, seg_ext, row_count):
    tap_count = taps_weight.shape[0]
    own_segment = seg_ext[tap_count - 1:]
    summed = jnp.zeros((row_count, extended.shape[1]), jnp.float32)
    for tap_index in range(tap_count):
        window = extended[tap_index:tap_index + row_count].astype(jnp.float32)
        keep_mask = (seg_ext[tap_index:tap_index + row_count] == own_segment).astype(jnp.float32)[:, None]
        summed = summed + taps_weight[tap_index].astype(jnp.float32)[None, :] * window * keep_mask
    return jax.nn.silu(summed).astype(jnp.bfloat16)


def block_terms(b_rows, c_rows, x_rows, decay_rows, step_rows, segments, seg_before):
    block_len = b_rows.shape[0]
    head_total = decay_rows.shape[0]
    x_heads = x_rows.reshape(block_len, head_total, -1)
    cumulative = jnp.cumsum(decay_rows, axis=1)
    products = jnp.dot(c_rows, b_rows.T, preferred_element_type=jnp.float32)
    local_index = jnp.arange(block_len)
    allowed = (local_index[None, :] <= local_index[:, None]) & (segments[None, :] == segments[:, None])
    spread = cumulative[:, :, None] - cumulative[:, None, :]
    decay_mat = jnp.where(allowed[None], jnp.exp(jnp.where(allowed[None], spread, 0.0)), 0.0)
    scores = (products[None] * decay_mat * step_rows[:, None, :]).astype(jnp.bfloat16)
    y_inner = jnp.einsum("hij,jhp->ihp", scores, x_heads, preferred_element_type=jnp.float32)
    ending = cumulative[:, -1]
    trailing = jnp.where((segments == segments[-1])[None, :], jnp.exp(ending[:, None] - cumulative), 0.0) * step_rows
    weighted = (trailing.T[:, :, None] * x_heads.astype(jnp.float32)).astype(jnp.bfloat16)
    local_state = jnp.einsum("jn,jhp->hnp", b_rows, weighted, preferred_element_type=jnp.float32)
    factor = jnp.where(segments[-1] == seg_before, jnp.exp(ending), 0.0)
    entry_gain = jnp.where((segments == seg_before)[None, :], jnp.exp(cumulative), 0.0)
    return y_inner.reshape(block_len, -1), local_state, factor, entry_gain


def local_pass(state_cols, value_cols, decay_cols, step_cols, seg_rows, seg_before, block_len):
    block_count = state_cols.shape[0] // block_len
    state_dim = state_cols.shape[1] // 2
    head_total = decay_cols.shape[1]
    b_all = state_cols[:, :state_dim].reshape(block_count, block_len, state_dim)
    c_all = state_cols[:, state_dim:].reshape(block_count, block_len, state_dim)
    x_all = value_cols.reshape(block_count, block_len, -1)
    decay_all = decay_cols.reshape(block_count, block_len, head_total).transpose(0, 2, 1)
    step_all = step_cols.reshape(block_count, block_len, head_total).transpose(0, 2, 1)
    seg_all = seg_rows.reshape(block_count, block_len)

    def one_block(block_item):
        return block_terms(*block_item)

    outputs = lax.map(one_block, (b_all, c_all, x_all, decay_all, step_all, seg_all, seg_before))
    return outputs, c_all


def prefix_blocks(local_state, factor):
    def chain_step(carry_pair, block_item):
        running, running_gain = carry_pair
        local_term, factor_term = block_item
        return (factor_term[:, None, None] * running + local_term, factor_term * running_gain), (running, running_gain)

    initial = (jnp.zeros(local_state.shape[1:], jnp.float32), jnp.ones((factor.shape[1],), jnp.float32))
    (shard_state, shard_gain), (inside, gain_list) = lax.scan(chain_step, initial, (local_state, factor))
    return shard_state, shard_gain, inside, gain_list


def finish(y_inner, incoming, entry_gain, c_all, value_cols, gate_cols):
    block_count, block_len, _ = y_inner.shape
    head_total = incoming.shape[1]
    carried = jnp.einsum("cin,chnp->cihp", c_all.astype(jnp.float32), incoming, precision=lax.Precision.HIGHEST)
    carried = carried * entry_gain.transpose(0, 2, 1)[:, :, :, None]
    x_heads = value_cols.reshape(block_count, block_len, head_total, -1).astype(jnp.float32)
    summed = y_inner.reshape(block_count, block_len, head_total, -1) + carried + x_heads
    gating = jax.nn.silu(gate_cols.astype(jnp.float32)).reshape(block_count, block_len, head_total, -1)
    return (summed * gating).reshape(block_count * block_len, -1).astype(jnp.bfloat16)


def reference(tokens, doc_lengths, value_weight, gate_weight, state_weight, step_weight, value_conv, state_conv, step_bias, log_rate):
    tap_count = CONV
    starts = (jnp.cumsum(doc_lengths) - doc_lengths).astype(jnp.int32)
    positions = jnp.arange(-(tap_count - 1), TOKENS).astype(jnp.int32)
    seg_ext = segment_of(positions, starts)
    state_flat = state_weight.transpose(1, 0, 2).reshape(D, GROUPS * 2 * STATE)
    value_proj = jnp.dot(tokens, value_weight, preferred_element_type=jnp.float32).astype(jnp.bfloat16)
    gate_proj = jnp.dot(tokens, gate_weight, preferred_element_type=jnp.float32).astype(jnp.bfloat16)
    state_proj = jnp.dot(tokens, state_flat, preferred_element_type=jnp.float32).astype(jnp.bfloat16)
    step_proj = jnp.dot(tokens, step_weight, preferred_element_type=jnp.float32).astype(jnp.bfloat16)
    value_ext = jnp.concatenate([jnp.zeros((tap_count - 1, value_proj.shape[1]), jnp.bfloat16), value_proj], axis=0)
    state_ext = jnp.concatenate([jnp.zeros((tap_count - 1, state_proj.shape[1]), jnp.bfloat16), state_proj], axis=0)
    value_act = causal_conv(value_ext, value_conv, seg_ext, TOKENS)
    conv_flat = state_conv.transpose(1, 0, 2).reshape(tap_count, GROUPS * 2 * STATE)
    state_act = causal_conv(state_ext, conv_flat, seg_ext, TOKENS)
    step_size = jax.nn.softplus(step_proj.astype(jnp.float32) + step_bias[None, :])
    decay_rate = -jnp.exp(log_rate)[None, :] * step_size
    seg_rows = seg_ext[tap_count - 1:]
    seg_before = seg_ext[tap_count - 2:tap_count - 2 + TOKENS:BLOCK]
    per_group = HEADS // GROUPS

    def group_out(group_index):
        state_cols = lax.dynamic_slice_in_dim(state_act, group_index * 2 * STATE, 2 * STATE, 1)
        value_cols = lax.dynamic_slice_in_dim(value_act, group_index * per_group * HEAD_DIM, per_group * HEAD_DIM, 1)
        gate_cols = lax.dynamic_slice_in_dim(gate_proj, group_index * per_group * HEAD_DIM, per_group * HEAD_DIM, 1)
        decay_cols = lax.dynamic_slice_in_dim(decay_rate, group_index * per_group, per_group, 1)
        step_cols = lax.dynamic_slice_in_dim(step_size, group_index * per_group, per_group, 1)
        (y_inner, local_state, factor, entry_gain), c_all = local_pass(state_cols, value_cols, decay_cols, step_cols, seg_rows, seg_before, BLOCK)
        shard_state, shard_gain, inside, gain_list = prefix_blocks(local_state, factor)
        return finish(y_inner, inside, entry_gain, c_all, value_cols, gate_cols)

    blocks = lax.map(group_out, jnp.arange(GROUPS).astype(jnp.int32))
    return blocks.transpose(1, 0, 2).reshape(TOKENS, HEADS * HEAD_DIM)
```

```python
import functools

import jax
import jax.numpy as jnp
from jax import lax
from jax.experimental import pallas as pl
from jax.experimental.pallas import tpu as pltpu
from jax.sharding import PartitionSpec as P

HEADS = 128
GROUPS = 8
BLOCK = 256


def passed_along(value, axis, steps):
    count = lax.axis_size(axis)
    leading, last = (max(0, -steps), min(count, count - steps))
    return lax.ppermute(value, axis, [(source, source + steps) for source in range(leading, last)])


def segment_of(positions, starts):
    reached = (starts[None, :] <= positions[:, None]).astype(jnp.int32)
    return jnp.sum(reached, axis=1) - 1


def causal_conv(extended, taps_weight, seg_ext, row_count):
    tap_count = taps_weight.shape[0]
    own_segment = seg_ext[tap_count - 1 :]
    summed = jnp.zeros((row_count, extended.shape[1]), jnp.float32)
    for tap_index in range(tap_count):
        window = extended[tap_index : tap_index + row_count].astype(jnp.float32)
        keep_mask = (seg_ext[tap_index : tap_index + row_count] == own_segment).astype(jnp.float32)[
            :, None
        ]
        summed = summed + taps_weight[tap_index][None, :] * window * keep_mask
    return jax.nn.silu(summed).astype(jnp.bfloat16)


def block_terms(b_rows, c_rows, x_rows, decay_rows, step_rows, segments, seg_before):
    block_len = b_rows.shape[0]
    head_total = decay_rows.shape[0]
    x_heads = x_rows.reshape(block_len, head_total, -1)
    cumulative = jnp.cumsum(decay_rows, axis=1)
    products = jnp.dot(c_rows, b_rows.T, preferred_element_type=jnp.float32)
    local_index = jnp.arange(block_len)
    allowed = (local_index[None, :] <= local_index[:, None]) & (
        segments[None, :] == segments[:, None]
    )
    spread = cumulative[:, :, None] - cumulative[:, None, :]
    decay_mat = jnp.where(allowed[None], jnp.exp(jnp.where(allowed[None], spread, 0.0)), 0.0)
    scores = (products[None] * decay_mat * step_rows[:, None, :]).astype(jnp.bfloat16)
    y_inner = jnp.einsum("hij,jhp->ihp", scores, x_heads, preferred_element_type=jnp.float32)
    ending = cumulative[:, -1]
    trailing = (
        jnp.where((segments == segments[-1])[None, :], jnp.exp(ending[:, None] - cumulative), 0.0)
        * step_rows
    )
    weighted = (trailing.T[:, :, None] * x_heads.astype(jnp.float32)).astype(jnp.bfloat16)
    local_state = jnp.einsum("jn,jhp->hnp", b_rows, weighted, preferred_element_type=jnp.float32)
    factor = jnp.where(segments[-1] == seg_before, jnp.exp(ending), 0.0)
    entry_gain = jnp.where((segments == seg_before)[None, :], jnp.exp(cumulative), 0.0)
    return (y_inner.reshape(block_len, -1), local_state, factor, entry_gain)


def local_pass(state_cols, value_cols, decay_cols, step_cols, seg_rows, seg_before, block_len):
    block_count = state_cols.shape[0] // block_len
    state_dim = state_cols.shape[1] // 2
    head_total = decay_cols.shape[1]
    b_all = state_cols[:, :state_dim].reshape(block_count, block_len, state_dim)
    c_all = state_cols[:, state_dim:].reshape(block_count, block_len, state_dim)
    x_all = value_cols.reshape(block_count, block_len, -1)
    decay_all = decay_cols.reshape(block_count, block_len, head_total).transpose(0, 2, 1)
    step_all = step_cols.reshape(block_count, block_len, head_total).transpose(0, 2, 1)
    seg_all = seg_rows.reshape(block_count, block_len)

    def one_block(block_item):
        return block_terms(*block_item)

    outputs = lax.map(one_block, (b_all, c_all, x_all, decay_all, step_all, seg_all, seg_before))
    return (outputs, c_all)


def prefix_blocks(local_state, factor):

    def chain_step(carry_pair, block_item):
        running, running_gain = carry_pair
        local_term, factor_term = block_item
        return (
            (factor_term[:, None, None] * running + local_term, factor_term * running_gain),
            (running, running_gain),
        )

    initial = (
        jnp.zeros(local_state.shape[1:], jnp.float32),
        jnp.ones((factor.shape[1],), jnp.float32),
    )
    (shard_state, shard_gain), (inside, gain_list) = lax.scan(
        chain_step, initial, (local_state, factor)
    )
    return (shard_state, shard_gain, inside, gain_list)


def finish(y_inner, incoming, entry_gain, c_all, value_cols, gate_cols):
    block_count, block_len, _ = y_inner.shape
    head_total = incoming.shape[1]
    carried = jnp.einsum(
        "cin,chnp->cihp", c_all.astype(jnp.float32), incoming, precision=lax.Precision.HIGHEST
    )
    carried = carried * entry_gain.transpose(0, 2, 1)[:, :, :, None]
    x_heads = value_cols.reshape(block_count, block_len, head_total, -1).astype(jnp.float32)
    summed = y_inner.reshape(block_count, block_len, head_total, -1) + carried + x_heads
    gating = jax.nn.silu(gate_cols.astype(jnp.float32)).reshape(
        block_count, block_len, head_total, -1
    )
    return (summed * gating).reshape(block_count * block_len, -1).astype(jnp.bfloat16)


def local(
    tokens,
    doc_lengths,
    value_weight,
    gate_weight,
    state_weight,
    step_weight,
    value_conv,
    state_conv,
    step_bias,
    log_rate,
):
    tok_dev = tokens.shape[0] * lax.axis_size("head")
    heads_here = step_weight.shape[1]
    tap_count = value_conv.shape[0]
    group_index = lax.axis_index("head") * heads_here // (HEADS // GROUPS)
    state_own = lax.dynamic_index_in_dim(state_weight, group_index, 0, keepdims=False)
    conv_own = lax.dynamic_index_in_dim(state_conv, group_index, 0, keepdims=False)
    gathered = lax.all_gather(tokens, "head", axis=0, tiled=True)
    shard_pieces = (
        lax.all_gather(value_weight, "seq", axis=0, tiled=True),
        lax.all_gather(gate_weight, "seq", axis=0, tiled=True),
        lax.all_gather(state_own, "seq", axis=0, tiled=True),
        lax.all_gather(step_weight, "seq", axis=0, tiled=True),
    )
    projected = tuple(
        (
            jnp.dot(gathered, weight_piece, preferred_element_type=jnp.float32)
            for weight_piece in shard_pieces
        )
    )
    value_proj = projected[0].astype(jnp.bfloat16)
    gate_proj = projected[1].astype(jnp.bfloat16)
    state_proj = projected[2].astype(jnp.bfloat16)
    step_proj = projected[3].astype(jnp.bfloat16)
    value_cols = value_proj.shape[1]
    rim_source = jnp.concatenate(
        [value_proj[-(tap_count - 1) :], state_proj[-(tap_count - 1) :]], axis=1
    )
    rim_rows = passed_along(rim_source, "seq", 1)
    value_ext = jnp.concatenate([rim_rows[:, :value_cols], value_proj], axis=0)
    state_ext = jnp.concatenate([rim_rows[:, value_cols:], state_proj], axis=0)
    starts = jnp.cumsum(doc_lengths) - doc_lengths
    positions = lax.axis_index("seq") * tok_dev + jnp.arange(-(tap_count - 1), tok_dev)
    seg_ext = segment_of(positions, starts)
    value_act = causal_conv(value_ext, value_conv, seg_ext, tok_dev)
    state_act = causal_conv(state_ext, conv_own, seg_ext, tok_dev)
    step_size = jax.nn.softplus(step_proj.astype(jnp.float32) + step_bias[None, :])
    decay_rate = -jnp.exp(log_rate)[None, :] * step_size
    seg_rows = seg_ext[tap_count - 1 :]
    seg_before = seg_ext[tap_count - 2 : tap_count - 2 + tok_dev : BLOCK]
    (y_inner, local_state, factor, entry_gain), c_all = local_pass(
        state_act, value_act, decay_rate, step_size, seg_rows, seg_before, BLOCK
    )
    shard_state, shard_gain, inside, gain_list = prefix_blocks(local_state, factor)

    def relay(step_index, arriving):
        leaving = shard_gain[:, None, None] * arriving + shard_state
        return passed_along(leaving, "seq", 1)

    entering = lax.fori_loop(0, lax.axis_size("seq") - 1, relay, jnp.zeros_like(shard_state))
    incoming = inside + gain_list[:, :, None, None] * entering[None]
    return finish(y_inner, incoming, entry_gain, c_all, value_act, gate_proj)


MESH = pl.DeviceIdType.MESH
SEQ_FAST, HEAD_FAST = 4, 8
F32 = jnp.float32
BF16 = jnp.bfloat16


def spread_kernel(tok, value_w, gate_w, state_w, step_w, tok_all, w_all, step_all,
                  tok_send, tok_recv, wt_send, wt_recv, own_sem):
    s = lax.axis_index("seq")
    h = lax.axis_index("head")
    y, x, c = h // 4, (h // 2) % 2, h % 2
    part = value_w.shape[0]
    cols = value_w.shape[1] // SEQ_FAST

    def head_of(yy, xx, cc):
        return yy * 4 + xx * 2 + cc

    mate, xnb, ynb = head_of(y, x, 1 - c), head_of(y, 1 - x, c), head_of(1 - y, x, c)
    barrier = pltpu.get_barrier_semaphore()
    for dist in range(1, SEQ_FAST):
        pl.semaphore_signal(barrier, inc=1, device_id=((s + dist) % SEQ_FAST, h), device_id_type=MESH)
    for nb in (mate, xnb, ynb):
        pl.semaphore_signal(barrier, inc=1, device_id=(s, nb), device_id_type=MESH)
    pl.semaphore_wait(barrier, SEQ_FAST + 2)

    def send(src, z, hh, to, kind):
        slot = z * HEAD_FAST + hh
        return pltpu.make_async_remote_copy(
            src_ref=src, dst_ref=tok_all.at[slot], send_sem=tok_send.at[kind, slot],
            recv_sem=tok_recv.at[slot], device_id=to, device_id_type=MESH)

    def arrived(z, hh):
        slot = z * HEAD_FAST + hh
        pltpu.make_async_remote_copy(
            src_ref=tok_all.at[slot], dst_ref=tok_all.at[slot], send_sem=tok_send.at[0, slot],
            recv_sem=tok_recv.at[slot], device_id=(s, mate), device_id_type=MESH).wait_recv()

    UP, DOWN, TOX, TOY, TOMATE = range(5)
    own = pltpu.make_async_copy(tok, tok_all.at[s * HEAD_FAST + h], own_sem.at[0])
    own.start()

    def plane(src, z):
        send(src, z, h, (s, xnb), TOX).start()
        send(src, z, h, (s, ynb), TOY).start()
        send(src, z, h, (s, mate), TOMATE).start()

    @pl.when(s < SEQ_FAST - 1)
    def _():
        send(tok, s, h, (s + 1, h), UP).start()

    @pl.when(s > 0)
    def _():
        send(tok, s, h, (s - 1, h), DOWN).start()

    plane(tok, s)

    def weights(dist):
        peer = (s + dist) % SEQ_FAST
        copies = []
        for which, ref in enumerate((value_w, gate_w)):
            src = ref.at[:, pl.ds(pl.multiple_of(peer * cols, cols), cols)]
            dst = w_all.at[pl.ds(pl.multiple_of(s * part, part), part), pl.ds(which * cols, cols)]
            copies.append((src, dst, which))
        copies.append((state_w.at[h], w_all.at[pl.ds(pl.multiple_of(s * part, part), part), pl.ds(2 * cols, state_w.shape[2])], 2))
        copies.append((step_w.at[peer], step_all.at[:, pl.ds(pl.multiple_of(s * part, part), part)], 3))
        if dist == 0:
            return [pltpu.make_async_copy(src, dst, own_sem.at[1 + which]) for src, dst, which in copies]
        return [pltpu.make_async_remote_copy(
            src_ref=src, dst_ref=dst, send_sem=wt_send.at[dist, which], recv_sem=wt_recv.at[dist, which],
            device_id=(peer, h), device_id_type=MESH) for src, dst, which in copies]

    own_weights = weights(0)
    for copy in own_weights:
        copy.start()

    for dist in range(1, SEQ_FAST):
        @pl.when(s - dist >= 0)
        def _():
            z = s - dist
            arrived(z, h)

            @pl.when(s < SEQ_FAST - 1)
            def _():
                send(tok_all.at[z * HEAD_FAST + h], z, h, (s + 1, h), UP).start()

            plane(tok_all.at[z * HEAD_FAST + h], z)

        @pl.when(s + dist < SEQ_FAST)
        def _():
            z = s + dist
            arrived(z, h)

            @pl.when(s > 0)
            def _():
                send(tok_all.at[z * HEAD_FAST + h], z, h, (s - 1, h), DOWN).start()

            plane(tok_all.at[z * HEAD_FAST + h], z)

    peer_weights = [weights(dist) for dist in range(1, SEQ_FAST)]
    for which in range(4):
        for copies in peer_weights:
            copies[which].start()

    def relay(z, hh, to, kind):
        slot = z * HEAD_FAST + hh
        send(tok_all.at[slot], z, hh, to, kind).start()

    for dist in range(SEQ_FAST):
        z = (s + dist) % SEQ_FAST
        arrived(z, xnb)
        if dist % 2 == 0:
            relay(z, xnb, (s, ynb), TOY)
        relay(z, xnb, (s, mate), TOMATE)
        arrived(z, ynb)
        if dist % 2 == 1:
            relay(z, ynb, (s, xnb), TOX)
        relay(z, ynb, (s, mate), TOMATE)
    diag = head_of(1 - y, 1 - x, c)
    for dist in range(SEQ_FAST):
        z = (s + dist) % SEQ_FAST
        arrived(z, diag)
        relay(z, diag, (s, mate), TOMATE)
    for dist in range(SEQ_FAST):
        z = (s + dist) % SEQ_FAST
        for yy, xx in ((y, x), (y, 1 - x), (1 - y, x), (1 - y, 1 - x)):
            arrived(z, head_of(yy, xx, 1 - c))

    for copies in peer_weights:
        for copy in copies:
            copy.wait()
    own.wait()
    for copy in own_weights:
        copy.wait()

    def sent(z, hh, kind):
        send(tok_all.at[z * HEAD_FAST + hh], z, hh, (s, mate), kind).wait_send()

    for z in range(SEQ_FAST):
        @pl.when((z <= s) & (s < SEQ_FAST - 1))
        def _():
            sent(z, h, UP)

        @pl.when((z >= s) & (s > 0))
        def _():
            sent(z, h, DOWN)

    for dist in range(SEQ_FAST):
        z = (s + dist) % SEQ_FAST
        sent(z, h, TOX)
        sent(z, h, TOY)
        for hh in (h, xnb, ynb, diag):
            sent(z, hh, TOMATE)
        if dist % 2 == 0:
            sent(z, xnb, TOY)
        else:
            sent(z, ynb, TOX)


def spread(tokens, value_weight, gate_weight, state_weight, step_parts):
    rows, width = tokens.shape
    part, wide = value_weight.shape
    cols = wide // SEQ_FAST
    any_spec = pl.BlockSpec(memory_space=pl.ANY)
    count = SEQ_FAST * HEAD_FAST
    return pl.pallas_call(
        spread_kernel,
        out_shape=(
            jax.ShapeDtypeStruct((count, rows, width), BF16),
            jax.ShapeDtypeStruct((part * SEQ_FAST, 2 * cols + state_weight.shape[2]), BF16),
            jax.ShapeDtypeStruct((step_parts.shape[1], part * SEQ_FAST), BF16),
        ),
        in_specs=[any_spec] * 5,
        out_specs=(any_spec,) * 3,
        scratch_shapes=[
            pltpu.SemaphoreType.DMA((5, count)),
            pltpu.SemaphoreType.DMA((count,)),
            pltpu.SemaphoreType.DMA((SEQ_FAST, 4)),
            pltpu.SemaphoreType.DMA((SEQ_FAST, 4)),
            pltpu.SemaphoreType.DMA((5,)),
        ],
        compiler_params=pltpu.CompilerParams(collective_id=0, has_side_effects=True),
        name="spread",
    )(tokens, value_weight, gate_weight, state_weight, step_parts)


def exact_dot(left, right, dims):
    return lax.dot_general(left, right, (dims, ((), ())), precision=lax.Precision.HIGHEST,
                           preferred_element_type=F32)


def fast_dot(left, right, dims=((1,), (0,))):
    return lax.dot_general(left, right, (dims, ((), ())), preferred_element_type=F32)


def silu(value):
    return value * lax.logistic(value)


def layer_kernel(heads_here, tok, w_all, step_all, seg_col, seg_row, before, taps, bias, rate,
                 out, carry, state):
    block = pl.program_id(0)
    block_len = tok.shape[0]
    cols = out.shape[1]
    chan = cols // heads_here
    state_dim = (w_all.shape[1] - 2 * cols) // 2
    tap_count = taps.shape[0]

    @pl.when(block == 0)
    def _():
        carry[...] = jnp.zeros_like(carry)
        state[...] = jnp.zeros_like(state)

    tokens = tok[...]
    proj = fast_dot(tokens, w_all[...]).astype(BF16)
    step_proj = fast_dot(tokens, step_all[...], ((1,), (1,))).astype(BF16).astype(F32)
    gate = proj[:, cols:2 * cols].astype(F32)
    conv_in = jnp.concatenate([proj[:, :cols], proj[:, 2 * cols:]], axis=1).astype(F32)
    segments = seg_col[...]
    tail = carry[...]
    carry[...] = conv_in[block_len - 8:]
    extended = jnp.concatenate([tail, conv_in], axis=0)
    summed = conv_in * taps[tap_count - 1:tap_count, :]
    for back in range(1, tap_count):
        window = extended[8 - back:8 - back + block_len]
        keep = segments[:, back:back + 1] > 0
        summed = summed + jnp.where(keep, taps[tap_count - 1 - back:tap_count - back, :] * window, 0.0)
    act = silu(summed).astype(BF16)
    x = act[:, :cols]
    b_rows = act[:, cols:cols + state_dim]
    c_rows = act[:, cols + state_dim:]

    raw = step_proj + bias[...]
    step = jnp.maximum(raw, 0.0) + jnp.log1p(jnp.exp(-jnp.abs(raw)))
    decay = -jnp.exp(rate[...]) * step
    row_id = lax.broadcasted_iota(jnp.int32, (block_len, block_len), 0)
    col_id = lax.broadcasted_iota(jnp.int32, (block_len, block_len), 1)
    lower = (col_id <= row_id)
    tri = lower.astype(F32)
    eye = (col_id == row_id).astype(F32)
    cum = exact_dot(tri, decay, ((1,), (0,)))
    cum_t = exact_dot(decay, tri, ((0,), (1,)))
    step_t = exact_dot(step, eye, ((0,), (0,)))
    allowed = lower & (seg_row[0] == segments[:, 0:1])
    products = jnp.where(allowed, fast_dot(c_rows, b_rows, ((1,), (1,))), 0.0)
    head_of_col = lax.broadcasted_iota(jnp.int32, (block_len, cols), 1) // chan
    xf = x.astype(F32)
    scores, x_parts = [], []
    for head in range(heads_here):
        spread_ij = jnp.where(lower, cum[:, head:head + 1] - cum_t[head:head + 1, :], 0.0)
        scores.append((products * jnp.exp(spread_ij) * step_t[head:head + 1, :]).astype(BF16))
        x_parts.append(jnp.where(head_of_col == head, xf, 0.0).astype(BF16))
    inner = fast_dot(jnp.concatenate(scores, axis=1), jnp.concatenate(x_parts, axis=0))

    width = step.shape[1]
    pick = (lax.broadcasted_iota(jnp.int32, (width, cols), 0)
            == lax.broadcasted_iota(jnp.int32, (width, cols), 1) // chan).astype(F32)
    seg_before = before[0][:, 0:1]
    last = segments[block_len - 1:block_len, 0:1]
    ending = cum[block_len - 1:block_len, :]
    same_last = segments[:, 0:1] == last
    same_before = segments[:, 0:1] == seg_before
    trailing = jnp.where(same_last, jnp.exp(ending - cum), 0.0) * step
    gain = jnp.where(same_before, jnp.exp(cum), 0.0)
    weighted = (exact_dot(trailing, pick, ((1,), (0,))) * xf).astype(BF16)
    gain_cols = exact_dot(gain, pick, ((1,), (0,)))
    factor = gain_cols[block_len - 1:block_len, :]
    entering = state[...]
    high = entering.astype(BF16)
    rest = entering - high.astype(F32)
    mid = rest.astype(BF16)
    low = (rest - mid.astype(F32)).astype(BF16)
    carried = fast_dot(c_rows, high) + fast_dot(c_rows, mid) + fast_dot(c_rows, low)
    state[...] = factor * entering + fast_dot(b_rows, weighted, ((0,), (0,)))
    total = inner + gain_cols * carried + xf
    out[...] = (total * silu(gate)).astype(BF16)


def layer(tok_all, w_all, step_all, seg_col, seg_row, before, taps, bias, rate, cols, heads_here, block_len):
    count = tok_all.shape[0] // block_len
    fixed = lambda array: pl.BlockSpec(array.shape, lambda i: (0,) * array.ndim)
    return pl.pallas_call(
        functools.partial(layer_kernel, heads_here),
        grid=(count,),
        out_shape=jax.ShapeDtypeStruct((tok_all.shape[0], cols), BF16),
        in_specs=[
            pl.BlockSpec((block_len, tok_all.shape[1]), lambda i: (i, 0)),
            fixed(w_all), fixed(step_all),
            pl.BlockSpec((block_len, seg_col.shape[1]), lambda i: (i, 0)),
            pl.BlockSpec((1, 1, block_len), lambda i: (i, 0, 0)),
            pl.BlockSpec((1, 1, before.shape[2]), lambda i: (i, 0, 0)),
            fixed(taps), fixed(bias), fixed(rate),
        ],
        out_specs=pl.BlockSpec((block_len, cols), lambda i: (i, 0)),
        scratch_shapes=[
            pltpu.VMEM((8, taps.shape[1]), F32),
            pltpu.VMEM(((w_all.shape[1] - 2 * cols) // 2, cols), F32),
        ],
        compiler_params=pltpu.CompilerParams(vmem_limit_bytes=48 * 1024 * 1024),
        name="layer",
    )(tok_all, w_all, step_all, seg_col, seg_row, before, taps, bias, rate)


def hand_out_kernel(mine, out, send_sem, recv_sem, own_sem):
    s = lax.axis_index("seq")
    h = lax.axis_index("head")
    rows = out.shape[0]
    cols = mine.shape[1]
    barrier = pltpu.get_barrier_semaphore()
    for dist in range(1, SEQ_FAST):
        pl.semaphore_signal(barrier, inc=1, device_id=((s + dist) % SEQ_FAST, h), device_id_type=MESH)
    pl.semaphore_wait(barrier, SEQ_FAST - 1)
    target = out.at[:, pl.ds(pl.multiple_of(s * cols, cols), cols)]
    copies = []
    for dist in range(1, SEQ_FAST):
        peer = (s + dist) % SEQ_FAST
        copies.append(pltpu.make_async_remote_copy(
            src_ref=mine.at[pl.ds(pl.multiple_of(peer * rows, rows), rows), :], dst_ref=target,
            send_sem=send_sem.at[dist], recv_sem=recv_sem.at[dist],
            device_id=(peer, h), device_id_type=MESH))
    copies.append(pltpu.make_async_copy(
        mine.at[pl.ds(pl.multiple_of(s * rows, rows), rows), :], target, own_sem))
    for copy in copies:
        copy.start()
    for copy in copies:
        copy.wait()


def hand_out(mine):
    any_spec = pl.BlockSpec(memory_space=pl.ANY)
    return pl.pallas_call(
        hand_out_kernel,
        out_shape=jax.ShapeDtypeStruct((mine.shape[0] // SEQ_FAST, mine.shape[1] * SEQ_FAST), BF16),
        in_specs=[any_spec],
        out_specs=any_spec,
        scratch_shapes=[
            pltpu.SemaphoreType.DMA((SEQ_FAST,)),
            pltpu.SemaphoreType.DMA((SEQ_FAST,)),
            pltpu.SemaphoreType.DMA,
        ],
        compiler_params=pltpu.CompilerParams(collective_id=1, has_side_effects=True),
        name="hand_out",
    )(mine)


def prepared(doc_lengths, value_conv, state_conv, step_bias, log_rate, total, cols, heads_here):
    s = lax.axis_index("seq")
    tap_count = value_conv.shape[0]
    conv_own = lax.dynamic_index_in_dim(state_conv, lax.axis_index("head"), 0, keepdims=False)
    taps = jnp.concatenate([lax.dynamic_slice_in_dim(value_conv, s * cols, cols, 1), conv_own], axis=1)
    starts = jnp.cumsum(doc_lengths) - doc_lengths
    seg_ext = segment_of(jnp.arange(-(tap_count - 1), total), starts)
    seg_rows = seg_ext[tap_count - 1:]
    same = [(seg_ext[tap_count - 1 - back:tap_count - 1 - back + total] == seg_rows).astype(jnp.int32)
            for back in range(1, tap_count)]
    seg_col = jnp.stack([seg_rows] + same, axis=1)
    seg_row = seg_rows.reshape(-1, 1, BLOCK)
    before = jnp.broadcast_to(seg_ext[tap_count - 2:tap_count - 2 + total:BLOCK][:, None, None],
                              (total // BLOCK, 1, 128))
    bias = lax.dynamic_slice_in_dim(step_bias, s * heads_here, heads_here, 0)
    rate = lax.dynamic_slice_in_dim(log_rate, s * heads_here, heads_here, 0)
    pad = (0, STEP_ROWS - heads_here)
    return taps, seg_col, seg_row, before, jnp.pad(bias, pad)[None], jnp.pad(rate, pad)[None]


STEP_ROWS = 16


def local_fast(tokens, doc_lengths, value_weight, gate_weight, state_weight, step_weight,
               value_conv, state_conv, step_bias, log_rate):
    total = tokens.shape[0] * SEQ_FAST * HEAD_FAST
    cols = value_weight.shape[1] // SEQ_FAST
    heads_here = step_weight.shape[1] // SEQ_FAST
    step_parts = step_weight.T.reshape(SEQ_FAST, heads_here, -1)
    step_parts = jnp.pad(step_parts, ((0, 0), (0, STEP_ROWS - heads_here), (0, 0)))
    small = prepared(doc_lengths, value_conv, state_conv, step_bias, log_rate, total, cols, heads_here)
    tok_all, w_all, step_all = spread(tokens, value_weight, gate_weight, state_weight, step_parts)
    taps, seg_col, seg_row, before, bias, rate = small
    mine = layer(tok_all.reshape(total, -1), w_all, step_all, seg_col, seg_row, before, taps, bias, rate,
                 cols, heads_here, BLOCK)
    return hand_out(mine)


def solution(mesh):
    fast = mesh.shape["seq"] == SEQ_FAST and mesh.shape["head"] == HEAD_FAST
    return jax.shard_map(
        local_fast if fast else local,
        mesh=mesh,
        in_specs=(
            P(("seq", "head"), None),
            P(),
            P("seq", "head"),
            P("seq", "head"),
            P(None, "seq", None),
            P("seq", "head"),
            P(None, "head"),
            P(),
            P("head"),
            P("head"),
        ),
        out_specs=P("seq", "head"),
        check_vma=False,
    )
```

```python
import functools

import jax
import jax.numpy as jnp
from jax import lax
from jax.experimental import pallas as pl
from jax.experimental.pallas import tpu as pltpu
from jax.sharding import PartitionSpec as P

HEADS = 128
GROUPS = 8
BLOCK = 256


def passed_along(value, axis, steps):
    count = lax.axis_size(axis)
    leading, last = (max(0, -steps), min(count, count - steps))
    return lax.ppermute(value, axis, [(source, source + steps) for source in range(leading, last)])


def segment_of(positions, starts):
    reached = (starts[None, :] <= positions[:, None]).astype(jnp.int32)
    return jnp.sum(reached, axis=1) - 1


def causal_conv(extended, taps_weight, seg_ext, row_count):
    tap_count = taps_weight.shape[0]
    own_segment = seg_ext[tap_count - 1 :]
    summed = jnp.zeros((row_count, extended.shape[1]), jnp.float32)
    for tap_index in range(tap_count):
        window = extended[tap_index : tap_index + row_count].astype(jnp.float32)
        keep_mask = (seg_ext[tap_index : tap_index + row_count] == own_segment).astype(jnp.float32)[
            :, None
        ]
        summed = summed + taps_weight[tap_index][None, :] * window * keep_mask
    return jax.nn.silu(summed).astype(jnp.bfloat16)


def block_terms(b_rows, c_rows, x_rows, decay_rows, step_rows, segments, seg_before):
    block_len = b_rows.shape[0]
    head_total = decay_rows.shape[0]
    x_heads = x_rows.reshape(block_len, head_total, -1)
    cumulative = jnp.cumsum(decay_rows, axis=1)
    products = jnp.dot(c_rows, b_rows.T, preferred_element_type=jnp.float32)
    local_index = jnp.arange(block_len)
    allowed = (local_index[None, :] <= local_index[:, None]) & (
        segments[None, :] == segments[:, None]
    )
    spread = cumulative[:, :, None] - cumulative[:, None, :]
    decay_mat = jnp.where(allowed[None], jnp.exp(jnp.where(allowed[None], spread, 0.0)), 0.0)
    scores = (products[None] * decay_mat * step_rows[:, None, :]).astype(jnp.bfloat16)
    y_inner = jnp.einsum("hij,jhp->ihp", scores, x_heads, preferred_element_type=jnp.float32)
    ending = cumulative[:, -1]
    trailing = (
        jnp.where((segments == segments[-1])[None, :], jnp.exp(ending[:, None] - cumulative), 0.0)
        * step_rows
    )
    weighted = (trailing.T[:, :, None] * x_heads.astype(jnp.float32)).astype(jnp.bfloat16)
    local_state = jnp.einsum("jn,jhp->hnp", b_rows, weighted, preferred_element_type=jnp.float32)
    factor = jnp.where(segments[-1] == seg_before, jnp.exp(ending), 0.0)
    entry_gain = jnp.where((segments == seg_before)[None, :], jnp.exp(cumulative), 0.0)
    return (y_inner.reshape(block_len, -1), local_state, factor, entry_gain)


def local_pass(state_cols, value_cols, decay_cols, step_cols, seg_rows, seg_before, block_len):
    block_count = state_cols.shape[0] // block_len
    state_dim = state_cols.shape[1] // 2
    head_total = decay_cols.shape[1]
    b_all = state_cols[:, :state_dim].reshape(block_count, block_len, state_dim)
    c_all = state_cols[:, state_dim:].reshape(block_count, block_len, state_dim)
    x_all = value_cols.reshape(block_count, block_len, -1)
    decay_all = decay_cols.reshape(block_count, block_len, head_total).transpose(0, 2, 1)
    step_all = step_cols.reshape(block_count, block_len, head_total).transpose(0, 2, 1)
    seg_all = seg_rows.reshape(block_count, block_len)

    def one_block(block_item):
        return block_terms(*block_item)

    outputs = lax.map(one_block, (b_all, c_all, x_all, decay_all, step_all, seg_all, seg_before))
    return (outputs, c_all)


def prefix_blocks(local_state, factor):

    def chain_step(carry_pair, block_item):
        running, running_gain = carry_pair
        local_term, factor_term = block_item
        return (
            (factor_term[:, None, None] * running + local_term, factor_term * running_gain),
            (running, running_gain),
        )

    initial = (
        jnp.zeros(local_state.shape[1:], jnp.float32),
        jnp.ones((factor.shape[1],), jnp.float32),
    )
    (shard_state, shard_gain), (inside, gain_list) = lax.scan(
        chain_step, initial, (local_state, factor)
    )
    return (shard_state, shard_gain, inside, gain_list)


def finish(y_inner, incoming, entry_gain, c_all, value_cols, gate_cols):
    block_count, block_len, _ = y_inner.shape
    head_total = incoming.shape[1]
    carried = jnp.einsum(
        "cin,chnp->cihp", c_all.astype(jnp.float32), incoming, precision=lax.Precision.HIGHEST
    )
    carried = carried * entry_gain.transpose(0, 2, 1)[:, :, :, None]
    x_heads = value_cols.reshape(block_count, block_len, head_total, -1).astype(jnp.float32)
    summed = y_inner.reshape(block_count, block_len, head_total, -1) + carried + x_heads
    gating = jax.nn.silu(gate_cols.astype(jnp.float32)).reshape(
        block_count, block_len, head_total, -1
    )
    return (summed * gating).reshape(block_count * block_len, -1).astype(jnp.bfloat16)


def local(
    tokens,
    doc_lengths,
    value_weight,
    gate_weight,
    state_weight,
    step_weight,
    value_conv,
    state_conv,
    step_bias,
    log_rate,
):
    tok_dev = tokens.shape[0] * lax.axis_size("head")
    heads_here = step_weight.shape[1]
    tap_count = value_conv.shape[0]
    group_index = lax.axis_index("head") * heads_here // (HEADS // GROUPS)
    state_own = lax.dynamic_index_in_dim(state_weight, group_index, 0, keepdims=False)
    conv_own = lax.dynamic_index_in_dim(state_conv, group_index, 0, keepdims=False)
    gathered = lax.all_gather(tokens, "head", axis=0, tiled=True)
    shard_pieces = (
        lax.all_gather(value_weight, "seq", axis=0, tiled=True),
        lax.all_gather(gate_weight, "seq", axis=0, tiled=True),
        lax.all_gather(state_own, "seq", axis=0, tiled=True),
        lax.all_gather(step_weight, "seq", axis=0, tiled=True),
    )
    projected = tuple(
        (
            jnp.dot(gathered, weight_piece, preferred_element_type=jnp.float32)
            for weight_piece in shard_pieces
        )
    )
    value_proj = projected[0].astype(jnp.bfloat16)
    gate_proj = projected[1].astype(jnp.bfloat16)
    state_proj = projected[2].astype(jnp.bfloat16)
    step_proj = projected[3].astype(jnp.bfloat16)
    value_cols = value_proj.shape[1]
    rim_source = jnp.concatenate(
        [value_proj[-(tap_count - 1) :], state_proj[-(tap_count - 1) :]], axis=1
    )
    rim_rows = passed_along(rim_source, "seq", 1)
    value_ext = jnp.concatenate([rim_rows[:, :value_cols], value_proj], axis=0)
    state_ext = jnp.concatenate([rim_rows[:, value_cols:], state_proj], axis=0)
    starts = jnp.cumsum(doc_lengths) - doc_lengths
    positions = lax.axis_index("seq") * tok_dev + jnp.arange(-(tap_count - 1), tok_dev)
    seg_ext = segment_of(positions, starts)
    value_act = causal_conv(value_ext, value_conv, seg_ext, tok_dev)
    state_act = causal_conv(state_ext, conv_own, seg_ext, tok_dev)
    step_size = jax.nn.softplus(step_proj.astype(jnp.float32) + step_bias[None, :])
    decay_rate = -jnp.exp(log_rate)[None, :] * step_size
    seg_rows = seg_ext[tap_count - 1 :]
    seg_before = seg_ext[tap_count - 2 : tap_count - 2 + tok_dev : BLOCK]
    (y_inner, local_state, factor, entry_gain), c_all = local_pass(
        state_act, value_act, decay_rate, step_size, seg_rows, seg_before, BLOCK
    )
    shard_state, shard_gain, inside, gain_list = prefix_blocks(local_state, factor)

    def relay(step_index, arriving):
        leaving = shard_gain[:, None, None] * arriving + shard_state
        return passed_along(leaving, "seq", 1)

    entering = lax.fori_loop(0, lax.axis_size("seq") - 1, relay, jnp.zeros_like(shard_state))
    incoming = inside + gain_list[:, :, None, None] * entering[None]
    return finish(y_inner, incoming, entry_gain, c_all, value_act, gate_proj)


MESH = pl.DeviceIdType.MESH
SEQ_FAST, HEAD_FAST = 4, 8
F32 = jnp.float32
BF16 = jnp.bfloat16


def spread_kernel(tok, value_w, gate_w, state_w, step_w, tok_all, w_all, step_all,
                  tok_send, tok_recv, wt_send, wt_recv, st_send, st_recv, own_sem):
    s = lax.axis_index("seq")
    h = lax.axis_index("head")
    y, x, c = h // 4, (h // 2) % 2, h % 2
    part = value_w.shape[0]
    cols = value_w.shape[1] // SEQ_FAST

    def head_of(yy, xx, cc):
        return yy * 4 + xx * 2 + cc

    mate, xnb, ynb = head_of(y, x, 1 - c), head_of(y, 1 - x, c), head_of(1 - y, x, c)
    barrier = pltpu.get_barrier_semaphore()
    for dist in range(1, SEQ_FAST):
        pl.semaphore_signal(barrier, inc=1, device_id=((s + dist) % SEQ_FAST, h), device_id_type=MESH)
    for nb in (mate, xnb, ynb):
        pl.semaphore_signal(barrier, inc=1, device_id=(s, nb), device_id_type=MESH)
    pl.semaphore_wait(barrier, SEQ_FAST + 2)

    def send(src, z, hh, to, kind):
        slot = z * HEAD_FAST + hh
        return pltpu.make_async_remote_copy(
            src_ref=src, dst_ref=tok_all.at[slot], send_sem=tok_send.at[kind, slot],
            recv_sem=tok_recv.at[slot], device_id=to, device_id_type=MESH)

    def arrived(z, hh):
        slot = z * HEAD_FAST + hh
        pltpu.make_async_remote_copy(
            src_ref=tok_all.at[slot], dst_ref=tok_all.at[slot], send_sem=tok_send.at[0, slot],
            recv_sem=tok_recv.at[slot], device_id=(s, mate), device_id_type=MESH).wait_recv()

    UP, DOWN, TOX, TOY, TOMATE = range(5)
    own = pltpu.make_async_copy(tok, tok_all.at[s * HEAD_FAST + h], own_sem.at[0])
    own.start()

    def plane(src, z):
        send(src, z, h, (s, xnb), TOX).start()
        send(src, z, h, (s, ynb), TOY).start()
        send(src, z, h, (s, mate), TOMATE).start()

    @pl.when(s < SEQ_FAST - 1)
    def _():
        send(tok, s, h, (s + 1, h), UP).start()

    @pl.when(s > 0)
    def _():
        send(tok, s, h, (s - 1, h), DOWN).start()

    plane(tok, s)

    def weights(dist):
        peer = (s + dist) % SEQ_FAST
        copies = []
        for which, ref in enumerate((value_w, gate_w)):
            src = ref.at[:, pl.ds(pl.multiple_of(peer * cols, cols), cols)]
            dst = w_all.at[pl.ds(pl.multiple_of(s * part, part), part), pl.ds(which * cols, cols)]
            copies.append((src, dst, which))
        copies.append((step_w.at[peer], step_all.at[:, pl.ds(pl.multiple_of(s * part, part), part)], 2))
        if dist == 0:
            copies.append((state_w.at[h], w_all.at[pl.ds(pl.multiple_of(s * part, part), part), pl.ds(2 * cols, state_w.shape[2])], 3))
            return [pltpu.make_async_copy(src, dst, own_sem.at[1 + which]) for src, dst, which in copies]
        return [pltpu.make_async_remote_copy(
            src_ref=src, dst_ref=dst, send_sem=wt_send.at[dist, which], recv_sem=wt_recv.at[dist, which],
            device_id=(peer, h), device_id_type=MESH) for src, dst, which in copies]

    own_weights = weights(0)
    for copy in own_weights:
        copy.start()

    def state_send(src, z, to, way):
        return pltpu.make_async_remote_copy(
            src_ref=src, dst_ref=w_all.at[pl.ds(pl.multiple_of(z * part, part), part), pl.ds(2 * cols, state_w.shape[2])],
            send_sem=st_send.at[way, z], recv_sem=st_recv.at[z], device_id=to, device_id_type=MESH)

    def state_piece(z):
        return w_all.at[pl.ds(pl.multiple_of(z * part, part), part), pl.ds(2 * cols, state_w.shape[2])]

    def both_sides(dist, act):
        @pl.when(s - dist >= 0)
        def _():
            act(s - dist, s < SEQ_FAST - 1, s + 1, UP)

        if dist > 0:
            @pl.when(s + dist < SEQ_FAST)
            def _():
                act(s + dist, s > 0, s - 1, DOWN)

    def token_round(z, onward, nxt, way):
        arrived(z, h)
        block = tok_all.at[z * HEAD_FAST + h]

        @pl.when(onward)
        def _():
            send(block, z, h, (nxt, h), way).start()

        plane(block, z)

    def state_round(z, onward, nxt, way):
        state_send(state_piece(z), z, (nxt, h), way).wait_recv()

        @pl.when(onward)
        def _():
            state_send(state_piece(z), z, (nxt, h), way).start()

    def relay(z, hh, to, kind):
        slot = z * HEAD_FAST + hh
        send(tok_all.at[slot], z, hh, to, kind).start()

    def plane_round(z, onward, nxt, way):
        arrived(z, xnb)

        @pl.when(z % 2 == 0)
        def _():
            relay(z, xnb, (s, ynb), TOY)

        relay(z, xnb, (s, mate), TOMATE)
        arrived(z, ynb)

        @pl.when(z % 2 == 1)
        def _():
            relay(z, ynb, (s, xnb), TOX)

        relay(z, ynb, (s, mate), TOMATE)

    both_sides(1, token_round)

    @pl.when(s < SEQ_FAST - 1)
    def _():
        state_send(state_w.at[h], s, (s + 1, h), UP).start()

    @pl.when(s > 0)
    def _():
        state_send(state_w.at[h], s, (s - 1, h), DOWN).start()

    both_sides(0, plane_round)
    both_sides(2, token_round)
    peer_weights = [weights(dist) for dist in range(1, SEQ_FAST)]
    for which in range(3):
        for copies in peer_weights:
            copies[which].start()
    both_sides(1, state_round)
    both_sides(1, plane_round)
    both_sides(3, token_round)
    both_sides(2, state_round)
    both_sides(2, plane_round)
    both_sides(3, state_round)
    both_sides(3, plane_round)
    diag = head_of(1 - y, 1 - x, c)
    for dist in range(SEQ_FAST):
        z = (s + dist) % SEQ_FAST
        arrived(z, diag)
        relay(z, diag, (s, mate), TOMATE)
    for dist in range(SEQ_FAST):
        z = (s + dist) % SEQ_FAST
        for yy, xx in ((y, x), (y, 1 - x), (1 - y, x), (1 - y, 1 - x)):
            arrived(z, head_of(yy, xx, 1 - c))

    for copies in peer_weights:
        for copy in copies:
            copy.wait()
    own.wait()
    for copy in own_weights:
        copy.wait()

    def sent(z, hh, kind):
        send(tok_all.at[z * HEAD_FAST + hh], z, hh, (s, mate), kind).wait_send()

    for z in range(SEQ_FAST):
        @pl.when((z <= s) & (s < SEQ_FAST - 1))
        def _():
            sent(z, h, UP)
            state_send(state_piece(z), z, (s, mate), UP).wait_send()

        @pl.when((z >= s) & (s > 0))
        def _():
            sent(z, h, DOWN)
            state_send(state_piece(z), z, (s, mate), DOWN).wait_send()

    for dist in range(SEQ_FAST):
        z = (s + dist) % SEQ_FAST
        sent(z, h, TOX)
        sent(z, h, TOY)
        for hh in (h, xnb, ynb, diag):
            sent(z, hh, TOMATE)

        @pl.when(z % 2 == 0)
        def _():
            sent(z, xnb, TOY)

        @pl.when(z % 2 == 1)
        def _():
            sent(z, ynb, TOX)


def spread(tokens, value_weight, gate_weight, state_weight, step_parts):
    rows, width = tokens.shape
    part, wide = value_weight.shape
    cols = wide // SEQ_FAST
    any_spec = pl.BlockSpec(memory_space=pl.ANY)
    count = SEQ_FAST * HEAD_FAST
    return pl.pallas_call(
        spread_kernel,
        out_shape=(
            jax.ShapeDtypeStruct((count, rows, width), BF16),
            jax.ShapeDtypeStruct((part * SEQ_FAST, 2 * cols + state_weight.shape[2]), BF16),
            jax.ShapeDtypeStruct((step_parts.shape[1], part * SEQ_FAST), BF16),
        ),
        in_specs=[any_spec] * 5,
        out_specs=(any_spec,) * 3,
        scratch_shapes=[
            pltpu.SemaphoreType.DMA((5, count)),
            pltpu.SemaphoreType.DMA((count,)),
            pltpu.SemaphoreType.DMA((SEQ_FAST, 3)),
            pltpu.SemaphoreType.DMA((SEQ_FAST, 3)),
            pltpu.SemaphoreType.DMA((2, SEQ_FAST)),
            pltpu.SemaphoreType.DMA((SEQ_FAST,)),
            pltpu.SemaphoreType.DMA((5,)),
        ],
        compiler_params=pltpu.CompilerParams(collective_id=0, has_side_effects=True),
        name="spread",
    )(tokens, value_weight, gate_weight, state_weight, step_parts)


def fast_dot(left, right, dims=((1,), (0,))):
    return lax.dot_general(left, right, (dims, ((), ())), preferred_element_type=F32)


def silu(value):
    return value * lax.logistic(value)


def parts_of(value):
    high = value.astype(BF16)
    rest = value - high.astype(F32)
    mid = rest.astype(BF16)
    return high, mid, (rest - mid.astype(F32)).astype(BF16)


def project(tokens, w_all, step_all, proj_to, step_to):
    proj_to[...] = fast_dot(tokens, w_all[...]).astype(BF16)
    step_to[...] = fast_dot(tokens, step_all[...], ((1,), (1,))).astype(BF16).astype(F32)


def one_block(heads_here, cols, proj, step_proj, segments, seg_row, seg_before, taps, bias, rate, carry, state):
    block_len = proj.shape[0]
    chan = cols // heads_here
    state_dim = (proj.shape[1] - 2 * cols) // 2
    tap_count = taps.shape[0]
    gate = proj[:, cols:2 * cols].astype(F32)
    conv_in = jnp.concatenate([proj[:, :cols], proj[:, 2 * cols:]], axis=1).astype(F32)
    tail = carry[...]
    carry[...] = conv_in[block_len - 8:]
    extended = jnp.concatenate([tail, conv_in], axis=0)
    summed = conv_in * taps[tap_count - 1:tap_count, :]
    for back in range(1, tap_count):
        window = extended[8 - back:8 - back + block_len]
        keep = segments[:, back:back + 1] > 0
        summed = summed + jnp.where(keep, taps[tap_count - 1 - back:tap_count - back, :] * window, 0.0)
    act = silu(summed).astype(BF16)
    x = act[:, :cols]
    b_rows = act[:, cols:cols + state_dim]
    c_rows = act[:, cols + state_dim:]

    raw = step_proj + bias
    step = jnp.maximum(raw, 0.0) + jnp.log1p(jnp.exp(-jnp.abs(raw)))
    width = step.shape[1]
    decay = -jnp.exp(rate) * step
    row_id = lax.broadcasted_iota(jnp.int32, (block_len, block_len), 0)
    col_id = lax.broadcasted_iota(jnp.int32, (block_len, block_len), 1)
    lower = col_id <= row_id
    sums = fast_dot(lower.astype(F32).astype(BF16), jnp.concatenate(parts_of(decay), axis=1))
    cum = sums[:, :width] + sums[:, width:2 * width] + sums[:, 2 * width:]
    turned = jnp.concatenate([cum, step], axis=1).T
    cum_t, step_t = turned[:width], turned[width:]
    allowed = lower & (seg_row == segments[:, 0:1])
    products = jnp.where(allowed, fast_dot(c_rows, b_rows, ((1,), (1,))), 0.0)
    head_of_col = lax.broadcasted_iota(jnp.int32, (block_len, cols), 1) // chan
    xf = x.astype(F32)
    scores, x_parts = [], []
    for head in range(heads_here):
        spread_ij = jnp.where(lower, cum[:, head:head + 1] - cum_t[head:head + 1, :], 0.0)
        scores.append((products * jnp.exp(spread_ij) * step_t[head:head + 1, :]).astype(BF16))
        x_parts.append(jnp.where(head_of_col == head, xf, 0.0).astype(BF16))
    inner = fast_dot(jnp.concatenate(scores, axis=1), jnp.concatenate(x_parts, axis=0))

    last = segments[block_len - 1:block_len, 0:1]
    ending = cum[block_len - 1:block_len, :]
    trailing = jnp.where(segments[:, 0:1] == last, jnp.exp(ending - cum), 0.0) * step
    gain = jnp.where(segments[:, 0:1] == seg_before, jnp.exp(cum), 0.0)
    pick_row = lax.broadcasted_iota(jnp.int32, (6 * width, 2 * cols), 0)
    pick_col = lax.broadcasted_iota(jnp.int32, (6 * width, 2 * cols), 1)
    pick = ((pick_row % width == (pick_col % cols) // chan)
            & (pick_row // (3 * width) == pick_col // cols)).astype(F32).astype(BF16)
    wide = fast_dot(jnp.concatenate(parts_of(trailing) + parts_of(gain), axis=1), pick)
    weighted = (wide[:, :cols] * xf).astype(BF16)
    gain_cols = wide[:, cols:]
    entering = state[...]
    high, mid, _ = parts_of(entering)
    carried = fast_dot(jnp.concatenate([c_rows, c_rows], axis=1), jnp.concatenate([high, mid], axis=0))
    state[...] = gain_cols[block_len - 1:block_len, :] * entering + fast_dot(b_rows, weighted, ((0,), (0,)))
    total = inner + gain_cols * carried + xf
    return (total * silu(gate)).astype(BF16)


def layer_kernel(heads_here, block_len, tok, w_all, step_all, seg_col_odd, seg_col_even, seg_row_odd, seg_row_even,
                 before_odd, before_even, taps, bias, rate, out,
                 carry, state, proj_even, step_even, proj_odd, step_odd, stage, send_sem, recv_sem, own_sem):
    step_id = pl.program_id(0)
    steps = pl.num_programs(0) - 1
    count = stage.shape[0]
    cols = stage.shape[2]
    per_peer = count // SEQ_FAST
    s = lax.axis_index("seq")
    h = lax.axis_index("head")

    def sending(block):
        return pltpu.make_async_remote_copy(
            src_ref=stage.at[block],
            dst_ref=out.at[pl.ds(pl.multiple_of((block % per_peer) * block_len, block_len), block_len),
                           pl.ds(pl.multiple_of(s * cols, cols), cols)],
            send_sem=send_sem.at[block], recv_sem=recv_sem.at[s, block % per_peer],
            device_id=(block // per_peer, h), device_id_type=MESH)

    def keeping(block):
        return pltpu.make_async_copy(
            stage.at[block],
            out.at[pl.ds(pl.multiple_of((block % per_peer) * block_len, block_len), block_len),
                   pl.ds(pl.multiple_of(s * cols, cols), cols)], own_sem.at[block % per_peer])

    def ship(block):
        @pl.when(block // per_peer != s)
        def _():
            sending(block).start()

        @pl.when(block // per_peer == s)
        def _():
            keeping(block).start()

    @pl.when(step_id == 0)
    def _():
        barrier = pltpu.get_barrier_semaphore()
        for dist in range(1, SEQ_FAST):
            pl.semaphore_signal(barrier, inc=1, device_id=((s + dist) % SEQ_FAST, h), device_id_type=MESH)
        pl.semaphore_wait(barrier, SEQ_FAST - 1)
        carry[...] = jnp.zeros_like(carry)
        state[...] = jnp.zeros_like(state)
        proj_odd[...] = jnp.zeros_like(proj_odd)
        step_odd[...] = jnp.zeros_like(step_odd)

    odd = jnp.maximum(2 * step_id - 1, 0)
    project(tok[:block_len], w_all, step_all, proj_even, step_even)
    stage[odd] = one_block(heads_here, cols, proj_odd[...], step_odd[...], seg_col_odd[...], seg_row_odd[0],
                           before_odd[0][:, 0:1], taps[...], bias[...], rate[...], carry, state)

    @pl.when(step_id > 0)
    def _():
        ship(2 * step_id - 1)

    @pl.when(step_id < steps)
    def _():
        project(tok[block_len:], w_all, step_all, proj_odd, step_odd)
        stage[2 * step_id] = one_block(
            heads_here, cols, proj_even[...], step_even[...], seg_col_even[...], seg_row_even[0],
            before_even[0][:, 0:1], taps[...], bias[...], rate[...], carry, state)
        ship(2 * step_id)

    @pl.when(step_id == steps)
    def _():
        for block in range(count):
            @pl.when(block // per_peer != s)
            def _():
                sending(block).wait_send()

            @pl.when(block // per_peer == s)
            def _():
                keeping(block).wait()

        for dist in range(1, SEQ_FAST):
            peer = (s + dist) % SEQ_FAST
            for index in range(per_peer):
                rows = pl.ds(index * block_len, block_len)
                there = out.at[rows, pl.ds(pl.multiple_of(peer * cols, cols), cols)]
                pltpu.make_async_remote_copy(
                    src_ref=there, dst_ref=there, send_sem=send_sem.at[0], recv_sem=recv_sem.at[peer, index],
                    device_id=(peer, h), device_id_type=MESH).wait_recv()


def layer(tok_all, w_all, step_all, seg_col, seg_row, before, taps, bias, rate, cols, heads_here, block_len):
    count = tok_all.shape[0] // block_len
    steps = count // 2
    fixed = lambda array: pl.BlockSpec(array.shape, lambda i: (0,) * array.ndim)
    odd = lambda i: jnp.maximum(2 * i - 1, 0)
    even = lambda i: jnp.minimum(2 * i, count - 2)
    return pl.pallas_call(
        functools.partial(layer_kernel, heads_here, block_len),
        grid=(steps + 1,),
        out_shape=jax.ShapeDtypeStruct((tok_all.shape[0] // SEQ_FAST, cols * SEQ_FAST), BF16),
        in_specs=[
            pl.BlockSpec((2 * block_len, tok_all.shape[1]), lambda i: (jnp.minimum(i, steps - 1), 0)),
            fixed(w_all), fixed(step_all),
            pl.BlockSpec((block_len, seg_col.shape[1]), lambda i: (odd(i), 0)),
            pl.BlockSpec((block_len, seg_col.shape[1]), lambda i: (even(i), 0)),
            pl.BlockSpec((1, 1, block_len), lambda i: (odd(i), 0, 0)),
            pl.BlockSpec((1, 1, block_len), lambda i: (even(i), 0, 0)),
            pl.BlockSpec((1, 1, before.shape[2]), lambda i: (odd(i), 0, 0)),
            pl.BlockSpec((1, 1, before.shape[2]), lambda i: (even(i), 0, 0)),
            fixed(taps), fixed(bias), fixed(rate),
        ],
        out_specs=pl.BlockSpec(memory_space=pl.ANY),
        scratch_shapes=[
            pltpu.VMEM((8, taps.shape[1]), F32),
            pltpu.VMEM(((w_all.shape[1] - 2 * cols) // 2, cols), F32),
            pltpu.VMEM((block_len, w_all.shape[1]), BF16),
            pltpu.VMEM((block_len, step_all.shape[0]), F32),
            pltpu.VMEM((block_len, w_all.shape[1]), BF16),
            pltpu.VMEM((block_len, step_all.shape[0]), F32),
            pltpu.VMEM((count, block_len, cols), BF16),
            pltpu.SemaphoreType.DMA((count,)),
            pltpu.SemaphoreType.DMA((SEQ_FAST, count // SEQ_FAST)),
            pltpu.SemaphoreType.DMA((count // SEQ_FAST,)),
        ],
        compiler_params=pltpu.CompilerParams(
            collective_id=1, has_side_effects=True, vmem_limit_bytes=56 * 1024 * 1024),
        name="layer",
    )(tok_all, w_all, step_all, seg_col, seg_col, seg_row, seg_row, before, before, taps, bias, rate)


def prepared(doc_lengths, value_conv, state_conv, step_bias, log_rate, total, cols, heads_here):
    s = lax.axis_index("seq")
    tap_count = value_conv.shape[0]
    conv_own = lax.dynamic_index_in_dim(state_conv, lax.axis_index("head"), 0, keepdims=False)
    taps = jnp.concatenate([lax.dynamic_slice_in_dim(value_conv, s * cols, cols, 1), conv_own], axis=1)
    starts = jnp.cumsum(doc_lengths) - doc_lengths
    seg_ext = segment_of(jnp.arange(-(tap_count - 1), total), starts)
    seg_rows = seg_ext[tap_count - 1:]
    same = [(seg_ext[tap_count - 1 - back:tap_count - 1 - back + total] == seg_rows).astype(jnp.int32)
            for back in range(1, tap_count)]
    seg_col = jnp.stack([seg_rows] + same, axis=1)
    seg_row = seg_rows.reshape(-1, 1, BLOCK)
    before = jnp.broadcast_to(seg_ext[tap_count - 2:tap_count - 2 + total:BLOCK][:, None, None],
                              (total // BLOCK, 1, 128))
    bias = lax.dynamic_slice_in_dim(step_bias, s * heads_here, heads_here, 0)
    rate = lax.dynamic_slice_in_dim(log_rate, s * heads_here, heads_here, 0)
    pad = (0, STEP_ROWS - heads_here)
    return taps, seg_col, seg_row, before, jnp.pad(bias, pad)[None], jnp.pad(rate, pad)[None]


STEP_ROWS = 16


def local_fast(tokens, doc_lengths, value_weight, gate_weight, state_weight, step_weight,
               value_conv, state_conv, step_bias, log_rate):
    total = tokens.shape[0] * SEQ_FAST * HEAD_FAST
    cols = value_weight.shape[1] // SEQ_FAST
    heads_here = step_weight.shape[1] // SEQ_FAST
    step_parts = step_weight.T.reshape(SEQ_FAST, heads_here, -1)
    step_parts = jnp.pad(step_parts, ((0, 0), (0, STEP_ROWS - heads_here), (0, 0)))
    small = prepared(doc_lengths, value_conv, state_conv, step_bias, log_rate, total, cols, heads_here)
    tok_all, w_all, step_all = spread(tokens, value_weight, gate_weight, state_weight, step_parts)
    taps, seg_col, seg_row, before, bias, rate = small
    return layer(tok_all.reshape(total, -1), w_all, step_all, seg_col, seg_row, before, taps, bias, rate,
                 cols, heads_here, BLOCK)


def solution(mesh):
    fast = mesh.shape["seq"] == SEQ_FAST and mesh.shape["head"] == HEAD_FAST
    return jax.shard_map(
        local_fast if fast else local,
        mesh=mesh,
        in_specs=(
            P(("seq", "head"), None),
            P(),
            P("seq", "head"),
            P("seq", "head"),
            P(None, "seq", None),
            P("seq", "head"),
            P(None, "head"),
            P(),
            P("head"),
            P("head"),
        ),
        out_specs=P("seq", "head"),
        check_vma=False,
    )
```

```python
import functools

import jax
import jax.numpy as jnp
import numpy as np
from jax import lax
from jax.experimental import pallas as pl
from jax.experimental.pallas import tpu as pltpu
from jax.sharding import PartitionSpec as P

HEADS = 128
GROUPS = 8
BLOCK = 256


def passed_along(value, axis, steps):
    count = lax.axis_size(axis)
    leading, last = (max(0, -steps), min(count, count - steps))
    return lax.ppermute(value, axis, [(source, source + steps) for source in range(leading, last)])


def segment_of(positions, starts):
    reached = (starts[None, :] <= positions[:, None]).astype(jnp.int32)
    return jnp.sum(reached, axis=1) - 1


def causal_conv(extended, taps_weight, seg_ext, row_count):
    tap_count = taps_weight.shape[0]
    own_segment = seg_ext[tap_count - 1 :]
    summed = jnp.zeros((row_count, extended.shape[1]), jnp.float32)
    for tap_index in range(tap_count):
        window = extended[tap_index : tap_index + row_count].astype(jnp.float32)
        keep_mask = (seg_ext[tap_index : tap_index + row_count] == own_segment).astype(jnp.float32)[
            :, None
        ]
        summed = summed + taps_weight[tap_index][None, :] * window * keep_mask
    return jax.nn.silu(summed).astype(jnp.bfloat16)


def block_terms(b_rows, c_rows, x_rows, decay_rows, step_rows, segments, seg_before):
    block_len = b_rows.shape[0]
    head_total = decay_rows.shape[0]
    x_heads = x_rows.reshape(block_len, head_total, -1)
    cumulative = jnp.cumsum(decay_rows, axis=1)
    products = jnp.dot(c_rows, b_rows.T, preferred_element_type=jnp.float32)
    local_index = jnp.arange(block_len)
    allowed = (local_index[None, :] <= local_index[:, None]) & (
        segments[None, :] == segments[:, None]
    )
    spread = cumulative[:, :, None] - cumulative[:, None, :]
    decay_mat = jnp.where(allowed[None], jnp.exp(jnp.where(allowed[None], spread, 0.0)), 0.0)
    scores = (products[None] * decay_mat * step_rows[:, None, :]).astype(jnp.bfloat16)
    y_inner = jnp.einsum("hij,jhp->ihp", scores, x_heads, preferred_element_type=jnp.float32)
    ending = cumulative[:, -1]
    trailing = (
        jnp.where((segments == segments[-1])[None, :], jnp.exp(ending[:, None] - cumulative), 0.0)
        * step_rows
    )
    weighted = (trailing.T[:, :, None] * x_heads.astype(jnp.float32)).astype(jnp.bfloat16)
    local_state = jnp.einsum("jn,jhp->hnp", b_rows, weighted, preferred_element_type=jnp.float32)
    factor = jnp.where(segments[-1] == seg_before, jnp.exp(ending), 0.0)
    entry_gain = jnp.where((segments == seg_before)[None, :], jnp.exp(cumulative), 0.0)
    return (y_inner.reshape(block_len, -1), local_state, factor, entry_gain)


def local_pass(state_cols, value_cols, decay_cols, step_cols, seg_rows, seg_before, block_len):
    block_count = state_cols.shape[0] // block_len
    state_dim = state_cols.shape[1] // 2
    head_total = decay_cols.shape[1]
    b_all = state_cols[:, :state_dim].reshape(block_count, block_len, state_dim)
    c_all = state_cols[:, state_dim:].reshape(block_count, block_len, state_dim)
    x_all = value_cols.reshape(block_count, block_len, -1)
    decay_all = decay_cols.reshape(block_count, block_len, head_total).transpose(0, 2, 1)
    step_all = step_cols.reshape(block_count, block_len, head_total).transpose(0, 2, 1)
    seg_all = seg_rows.reshape(block_count, block_len)

    def one_block(block_item):
        return block_terms(*block_item)

    outputs = lax.map(one_block, (b_all, c_all, x_all, decay_all, step_all, seg_all, seg_before))
    return (outputs, c_all)


def prefix_blocks(local_state, factor):

    def chain_step(carry_pair, block_item):
        running, running_gain = carry_pair
        local_term, factor_term = block_item
        return (
            (factor_term[:, None, None] * running + local_term, factor_term * running_gain),
            (running, running_gain),
        )

    initial = (
        jnp.zeros(local_state.shape[1:], jnp.float32),
        jnp.ones((factor.shape[1],), jnp.float32),
    )
    (shard_state, shard_gain), (inside, gain_list) = lax.scan(
        chain_step, initial, (local_state, factor)
    )
    return (shard_state, shard_gain, inside, gain_list)


def finish(y_inner, incoming, entry_gain, c_all, value_cols, gate_cols):
    block_count, block_len, _ = y_inner.shape
    head_total = incoming.shape[1]
    carried = jnp.einsum(
        "cin,chnp->cihp", c_all.astype(jnp.float32), incoming, precision=lax.Precision.HIGHEST
    )
    carried = carried * entry_gain.transpose(0, 2, 1)[:, :, :, None]
    x_heads = value_cols.reshape(block_count, block_len, head_total, -1).astype(jnp.float32)
    summed = y_inner.reshape(block_count, block_len, head_total, -1) + carried + x_heads
    gating = jax.nn.silu(gate_cols.astype(jnp.float32)).reshape(
        block_count, block_len, head_total, -1
    )
    return (summed * gating).reshape(block_count * block_len, -1).astype(jnp.bfloat16)


def local(
    tokens,
    doc_lengths,
    value_weight,
    gate_weight,
    state_weight,
    step_weight,
    value_conv,
    state_conv,
    step_bias,
    log_rate,
):
    tok_dev = tokens.shape[0] * lax.axis_size("head")
    heads_here = step_weight.shape[1]
    tap_count = value_conv.shape[0]
    group_index = lax.axis_index("head") * heads_here // (HEADS // GROUPS)
    state_own = lax.dynamic_index_in_dim(state_weight, group_index, 0, keepdims=False)
    conv_own = lax.dynamic_index_in_dim(state_conv, group_index, 0, keepdims=False)
    gathered = lax.all_gather(tokens, "head", axis=0, tiled=True)
    shard_pieces = (
        lax.all_gather(value_weight, "seq", axis=0, tiled=True),
        lax.all_gather(gate_weight, "seq", axis=0, tiled=True),
        lax.all_gather(state_own, "seq", axis=0, tiled=True),
        lax.all_gather(step_weight, "seq", axis=0, tiled=True),
    )
    projected = tuple(
        (
            jnp.dot(gathered, weight_piece, preferred_element_type=jnp.float32)
            for weight_piece in shard_pieces
        )
    )
    value_proj = projected[0].astype(jnp.bfloat16)
    gate_proj = projected[1].astype(jnp.bfloat16)
    state_proj = projected[2].astype(jnp.bfloat16)
    step_proj = projected[3].astype(jnp.bfloat16)
    value_cols = value_proj.shape[1]
    rim_source = jnp.concatenate(
        [value_proj[-(tap_count - 1) :], state_proj[-(tap_count - 1) :]], axis=1
    )
    rim_rows = passed_along(rim_source, "seq", 1)
    value_ext = jnp.concatenate([rim_rows[:, :value_cols], value_proj], axis=0)
    state_ext = jnp.concatenate([rim_rows[:, value_cols:], state_proj], axis=0)
    starts = jnp.cumsum(doc_lengths) - doc_lengths
    positions = lax.axis_index("seq") * tok_dev + jnp.arange(-(tap_count - 1), tok_dev)
    seg_ext = segment_of(positions, starts)
    value_act = causal_conv(value_ext, value_conv, seg_ext, tok_dev)
    state_act = causal_conv(state_ext, conv_own, seg_ext, tok_dev)
    step_size = jax.nn.softplus(step_proj.astype(jnp.float32) + step_bias[None, :])
    decay_rate = -jnp.exp(log_rate)[None, :] * step_size
    seg_rows = seg_ext[tap_count - 1 :]
    seg_before = seg_ext[tap_count - 2 : tap_count - 2 + tok_dev : BLOCK]
    (y_inner, local_state, factor, entry_gain), c_all = local_pass(
        state_act, value_act, decay_rate, step_size, seg_rows, seg_before, BLOCK
    )
    shard_state, shard_gain, inside, gain_list = prefix_blocks(local_state, factor)

    def relay(step_index, arriving):
        leaving = shard_gain[:, None, None] * arriving + shard_state
        return passed_along(leaving, "seq", 1)

    entering = lax.fori_loop(0, lax.axis_size("seq") - 1, relay, jnp.zeros_like(shard_state))
    incoming = inside + gain_list[:, :, None, None] * entering[None]
    return finish(y_inner, incoming, entry_gain, c_all, value_act, gate_proj)


MESH = pl.DeviceIdType.MESH
SEQ_FAST, HEAD_FAST = 4, 8
F32 = jnp.float32
BF16 = jnp.bfloat16


def spread_kernel(tok, value_w, gate_w, state_w, step_w, tok_all, w_vs, w_gate, step_all, proj, step_proj,
                  tok_send, tok_recv, wt_send, wt_recv, st_send, st_recv, own_sem, vs_here, step_here, fetch_sem):
    s = lax.axis_index("seq")
    h = lax.axis_index("head")
    y, x, c = h // 4, (h // 2) % 2, h % 2
    part = value_w.shape[0]
    cols = value_w.shape[1] // SEQ_FAST

    def head_of(yy, xx, cc):
        return yy * 4 + xx * 2 + cc

    mate, xnb, ynb = head_of(y, x, 1 - c), head_of(y, 1 - x, c), head_of(1 - y, x, c)
    barrier = pltpu.get_barrier_semaphore()
    for dist in range(1, SEQ_FAST):
        pl.semaphore_signal(barrier, inc=1, device_id=((s + dist) % SEQ_FAST, h), device_id_type=MESH)
    for nb in (mate, xnb, ynb):
        pl.semaphore_signal(barrier, inc=1, device_id=(s, nb), device_id_type=MESH)
    pl.semaphore_wait(barrier, SEQ_FAST + 2)

    def send(src, z, hh, to, kind):
        slot = z * HEAD_FAST + hh
        return pltpu.make_async_remote_copy(
            src_ref=src, dst_ref=tok_all.at[slot], send_sem=tok_send.at[kind, slot],
            recv_sem=tok_recv.at[slot], device_id=to, device_id_type=MESH)

    def arrived(z, hh):
        slot = z * HEAD_FAST + hh
        pltpu.make_async_remote_copy(
            src_ref=tok_all.at[slot], dst_ref=tok_all.at[slot], send_sem=tok_send.at[0, slot],
            recv_sem=tok_recv.at[slot], device_id=(s, mate), device_id_type=MESH).wait_recv()

    UP, DOWN, TOX, TOY, TOMATE = range(5)
    own = pltpu.make_async_copy(tok, tok_all.at[s * HEAD_FAST + h], own_sem.at[0])
    own.start()

    def plane(src, z):
        send(src, z, h, (s, xnb), TOX).start()
        send(src, z, h, (s, ynb), TOY).start()
        send(src, z, h, (s, mate), TOMATE).start()

    @pl.when(s < SEQ_FAST - 1)
    def _():
        send(tok, s, h, (s + 1, h), UP).start()

    @pl.when(s > 0)
    def _():
        send(tok, s, h, (s - 1, h), DOWN).start()

    plane(tok, s)

    def weights(dist):
        peer = (s + dist) % SEQ_FAST
        copies = []
        for which, ref in enumerate((value_w, gate_w)):
            src = ref.at[:, pl.ds(pl.multiple_of(peer * cols, cols), cols)]
            dst = (w_vs, w_gate)[which].at[pl.ds(pl.multiple_of(s * part, part), part), pl.ds(0, cols)]
            copies.append((src, dst, which))
        copies.append((step_w.at[peer], step_all.at[:, pl.ds(pl.multiple_of(s * part, part), part)], 2))
        if dist == 0:
            copies.append((state_w.at[h], w_vs.at[pl.ds(pl.multiple_of(s * part, part), part), pl.ds(cols, state_w.shape[2])], 3))
            return [pltpu.make_async_copy(src, dst, own_sem.at[1 + which]) for src, dst, which in copies]
        return [pltpu.make_async_remote_copy(
            src_ref=src, dst_ref=dst, send_sem=wt_send.at[dist, which], recv_sem=wt_recv.at[dist, which],
            device_id=(peer, h), device_id_type=MESH) for src, dst, which in copies]

    own_weights = weights(0)
    for copy in own_weights:
        copy.start()

    def sent(z, hh, kind):
        send(tok_all.at[z * HEAD_FAST + hh], z, hh, (s, mate), kind).wait_send()

    def state_send(src, z, to, way):
        return pltpu.make_async_remote_copy(
            src_ref=src, dst_ref=w_vs.at[pl.ds(pl.multiple_of(z * part, part), part), pl.ds(cols, state_w.shape[2])],
            send_sem=st_send.at[way, z], recv_sem=st_recv.at[z], device_id=to, device_id_type=MESH)

    def state_piece(z):
        return w_vs.at[pl.ds(pl.multiple_of(z * part, part), part), pl.ds(cols, state_w.shape[2])]

    def both_sides(dist, act):
        @pl.when(s - dist >= 0)
        def _():
            act(s - dist, s < SEQ_FAST - 1, s + 1, UP)

        if dist > 0:
            @pl.when(s + dist < SEQ_FAST)
            def _():
                act(s + dist, s > 0, s - 1, DOWN)

    def token_round(z, onward, nxt, way):
        arrived(z, h)
        block = tok_all.at[z * HEAD_FAST + h]

        @pl.when(onward)
        def _():
            send(block, z, h, (nxt, h), way).start()

        plane(block, z)

    def state_round(z, onward, nxt, way):
        state_send(state_piece(z), z, (nxt, h), way).wait_recv()

        @pl.when(onward)
        def _():
            state_send(state_piece(z), z, (nxt, h), way).start()

    def relay(z, hh, to, kind):
        slot = z * HEAD_FAST + hh
        send(tok_all.at[slot], z, hh, to, kind).start()

    def plane_round(z, onward, nxt, way):
        arrived(z, xnb)

        @pl.when(z % 2 == 0)
        def _():
            relay(z, xnb, (s, ynb), TOY)

        relay(z, xnb, (s, mate), TOMATE)
        arrived(z, ynb)

        @pl.when(z % 2 == 1)
        def _():
            relay(z, ynb, (s, xnb), TOX)

        relay(z, ynb, (s, mate), TOMATE)

    def token_left(z, onward, nxt, way):
        @pl.when(onward)
        def _():
            sent(z, h, way)

    both_sides(1, token_round)
    both_sides(0, plane_round)
    both_sides(2, token_round)

    @pl.when(s < SEQ_FAST - 1)
    def _():
        state_send(state_w.at[h], s, (s + 1, h), UP).start()

    @pl.when(s > 0)
    def _():
        state_send(state_w.at[h], s, (s - 1, h), DOWN).start()

    both_sides(1, plane_round)
    both_sides(3, token_round)
    both_sides(1, state_round)
    both_sides(2, token_left)
    peer_weights = [weights(dist) for dist in range(1, SEQ_FAST)]
    for copies in peer_weights:
        copies[0].start()
        copies[2].start()
    both_sides(2, plane_round)
    both_sides(2, state_round)
    both_sides(3, plane_round)
    for copies in peer_weights:
        copies[0].wait_send()
    for copies in peer_weights:
        copies[1].start()
    diag = head_of(1 - y, 1 - x, c)
    for dist in range(SEQ_FAST):
        z = (s + dist) % SEQ_FAST
        arrived(z, diag)
        relay(z, diag, (s, mate), TOMATE)
    for dist in range(SEQ_FAST):
        z = (s + dist) % SEQ_FAST
        for yy, xx in ((y, x), (y, 1 - x), (1 - y, x), (1 - y, 1 - x)):
            arrived(z, head_of(yy, xx, 1 - c))

    both_sides(3, state_round)
    own.wait()
    for copy in own_weights:
        copy.wait()
    for copies in peer_weights:
        copies[0].wait_recv()
        copies[2].wait()
    fetches = [pltpu.make_async_copy(w_vs, vs_here, fetch_sem.at[0]),
               pltpu.make_async_copy(step_all, step_here, fetch_sem.at[1])]
    for copy in fetches:
        copy.start()
    for copy in fetches:
        copy.wait()

    def project(tokens, proj_to, step_to):
        rows = tokens[...].reshape(-1, tokens.shape[2])
        proj_to[...] = fast_dot(rows, vs_here[...]).astype(BF16)
        step_to[...] = fast_dot(rows, step_here[...], ((1,), (1,))).astype(BF16).astype(F32)

    count, rows, width = tok_all.shape
    pltpu.emit_pipeline(
        project, grid=(count // 2,),
        in_specs=[pl.BlockSpec((2, rows, width), lambda i: (i, 0, 0))],
        out_specs=[pl.BlockSpec((2 * rows, proj.shape[1]), lambda i: (i, 0)),
                   pl.BlockSpec((2 * rows, step_proj.shape[1]), lambda i: (i, 0))],
    )(tok_all, proj, step_proj)
    for copies in peer_weights:
        copies[1].wait()

    for z in range(SEQ_FAST):
        @pl.when((z <= s) & (s < SEQ_FAST - 1))
        def _():
            state_send(state_piece(z), z, (s, mate), UP).wait_send()

        @pl.when((z >= s) & (s > 0))
        def _():
            state_send(state_piece(z), z, (s, mate), DOWN).wait_send()

    @pl.when(s < SEQ_FAST - 1)
    def _():
        sent(s, h, UP)

    @pl.when(s > 0)
    def _():
        sent(s, h, DOWN)

    both_sides(1, token_left)
    both_sides(3, token_left)
    for dist in range(SEQ_FAST):
        z = (s + dist) % SEQ_FAST
        sent(z, h, TOX)
        sent(z, h, TOY)
        for hh in (h, xnb, ynb, diag):
            sent(z, hh, TOMATE)

        @pl.when(z % 2 == 0)
        def _():
            sent(z, xnb, TOY)

        @pl.when(z % 2 == 1)
        def _():
            sent(z, ynb, TOX)


def spread(tokens, value_weight, gate_weight, state_weight, step_parts):
    rows, width = tokens.shape
    part, wide = value_weight.shape
    cols = wide // SEQ_FAST
    any_spec = pl.BlockSpec(memory_space=pl.ANY)
    count = SEQ_FAST * HEAD_FAST
    return pl.pallas_call(
        spread_kernel,
        out_shape=(
            jax.ShapeDtypeStruct((count, rows, width), BF16),
            jax.ShapeDtypeStruct((part * SEQ_FAST, cols + state_weight.shape[2]), BF16),
            jax.ShapeDtypeStruct((part * SEQ_FAST, cols), BF16),
            jax.ShapeDtypeStruct((step_parts.shape[1], part * SEQ_FAST), BF16),
            jax.ShapeDtypeStruct((count * rows, cols + state_weight.shape[2]), BF16),
            jax.ShapeDtypeStruct((count * rows, step_parts.shape[1]), F32),
        ),
        in_specs=[any_spec] * 5,
        out_specs=(any_spec,) * 6,
        scratch_shapes=[
            pltpu.SemaphoreType.DMA((5, count)),
            pltpu.SemaphoreType.DMA((count,)),
            pltpu.SemaphoreType.DMA((SEQ_FAST, 3)),
            pltpu.SemaphoreType.DMA((SEQ_FAST, 3)),
            pltpu.SemaphoreType.DMA((2, SEQ_FAST)),
            pltpu.SemaphoreType.DMA((SEQ_FAST,)),
            pltpu.SemaphoreType.DMA((5,)),
            pltpu.VMEM((part * SEQ_FAST, cols + state_weight.shape[2]), BF16),
            pltpu.VMEM((step_parts.shape[1], part * SEQ_FAST), BF16),
            pltpu.SemaphoreType.DMA((2,)),
        ],
        compiler_params=pltpu.CompilerParams(
            collective_id=0, has_side_effects=True, vmem_limit_bytes=32 * 1024 * 1024),
        name="spread",
    )(tokens, value_weight, gate_weight, state_weight, step_parts)


def fast_dot(left, right, dims=((1,), (0,))):
    return lax.dot_general(left, right, (dims, ((), ())), preferred_element_type=F32)


def silu(value):
    return value * lax.logistic(value)


def parts_of(value):
    high = value.astype(BF16)
    rest = value - high.astype(F32)
    mid = rest.astype(BF16)
    return high, mid, (rest - mid.astype(F32)).astype(BF16)


def one_block(heads_here, cols, proj, step_proj, gate, segments, seg_row, taps, bias, rate, pick, carry, state):
    block_len = proj.shape[0]
    half = block_len // 2
    chan = cols // heads_here
    state_dim = (proj.shape[1] - cols) // 2
    tap_count = taps.shape[0]
    conv_in = proj.astype(F32)
    tail = carry[...]
    carry[...] = conv_in[block_len - 8:]
    extended = jnp.concatenate([tail, conv_in], axis=0)
    summed = conv_in * taps[tap_count - 1:tap_count, :]
    own = segments[:, 0:1]
    for back in range(1, tap_count):
        window = extended[8 - back:8 - back + block_len]
        keep = segments[:, back:back + 1] == own
        summed = summed + jnp.where(keep, taps[tap_count - 1 - back:tap_count - back, :] * window, 0.0)
    act = silu(summed).astype(BF16)
    x = act[:, :cols]
    b_rows = act[:, cols:cols + state_dim]
    c_rows = act[:, cols + state_dim:]

    raw = step_proj + bias
    step = jnp.maximum(raw, 0.0) + jnp.log1p(jnp.exp(-jnp.abs(raw)))
    width = step.shape[1]
    decay = -jnp.exp(rate) * step
    row_id = lax.broadcasted_iota(jnp.int32, (block_len, block_len), 0)
    col_id = lax.broadcasted_iota(jnp.int32, (block_len, block_len), 1)
    lower = col_id <= row_id
    sums = fast_dot(lower.astype(F32).astype(BF16), jnp.concatenate(parts_of(decay), axis=1))
    cum = sums[:, :width] + sums[:, width:2 * width] + sums[:, 2 * width:]
    turned = jnp.concatenate([cum, step], axis=1).T
    cum_t, step_t = turned[:width], turned[width:]
    allowed = lower & (seg_row == own)
    products = jnp.where(allowed, fast_dot(c_rows, b_rows, ((1,), (1,))), 0.0)
    head_of_col = lax.broadcasted_iota(jnp.int32, (1, cols), 1) // chan
    xf = x.astype(F32)
    x_parts = [jnp.where(head_of_col == head, xf, 0.0).astype(BF16) for head in range(heads_here)]

    def rows_of(first, rows, upto):
        scores = []
        for head in range(heads_here):
            spread_ij = jnp.minimum(cum[first:first + rows, head:head + 1] - cum_t[head:head + 1, :upto], 0.0)
            scores.append((products[first:first + rows, :upto] * jnp.exp(spread_ij)
                           * step_t[head:head + 1, :upto]).astype(BF16))
        return fast_dot(jnp.concatenate(scores, axis=1), jnp.concatenate([xp[:upto] for xp in x_parts], axis=0))

    inner = jnp.concatenate([rows_of(0, half, half), rows_of(half, half, block_len)], axis=0)

    ending = cum[block_len - 1:block_len, :]
    trailing = jnp.where(own == own[block_len - 1:block_len], jnp.exp(ending - cum), 0.0) * step
    gain = jnp.where(own == segments[0:1, 1:2], jnp.exp(cum), 0.0)
    wide = fast_dot(jnp.concatenate(parts_of(trailing) + parts_of(gain), axis=1), pick)
    weighted = (wide[:, :cols] * xf).astype(BF16)
    gain_cols = wide[:, cols:]
    entering = state[...]
    high, mid, _ = parts_of(entering)
    carried = fast_dot(jnp.concatenate([c_rows, c_rows], axis=1), jnp.concatenate([high, mid], axis=0))
    state[...] = gain_cols[block_len - 1:block_len, :] * entering + fast_dot(b_rows, weighted, ((0,), (0,)))
    total = inner + gain_cols * carried + xf
    return (total * silu(gate)).astype(BF16)


def layer_kernel(heads_here, tok, w_gate, proj, step_proj, segs, value_taps, state_taps, head_terms, pick, out,
                 carry, state, stage, send_sem, recv_sem, own_sem):
    block = pl.program_id(0)
    count = stage.shape[0]
    block_len, cols = stage.shape[1:]
    per_peer = count // SEQ_FAST
    s = lax.axis_index("seq")
    h = lax.axis_index("head")

    def sending(index):
        return pltpu.make_async_remote_copy(
            src_ref=stage.at[index],
            dst_ref=out.at[pl.ds(pl.multiple_of((index % per_peer) * block_len, block_len), block_len),
                           pl.ds(pl.multiple_of(s * cols, cols), cols)],
            send_sem=send_sem.at[index], recv_sem=recv_sem.at[s, index % per_peer],
            device_id=(index // per_peer, h), device_id_type=MESH)

    def keeping(index):
        return pltpu.make_async_copy(
            stage.at[index],
            out.at[pl.ds(pl.multiple_of((index % per_peer) * block_len, block_len), block_len),
                   pl.ds(pl.multiple_of(s * cols, cols), cols)], own_sem.at[index % per_peer])

    @pl.when(block == 0)
    def _():
        barrier = pltpu.get_barrier_semaphore()
        for dist in range(1, SEQ_FAST):
            pl.semaphore_signal(barrier, inc=1, device_id=((s + dist) % SEQ_FAST, h), device_id_type=MESH)
        pl.semaphore_wait(barrier, SEQ_FAST - 1)
        carry[...] = jnp.zeros_like(carry)
        state[...] = jnp.zeros_like(state)

    gate = fast_dot(tok[...], w_gate[...]).astype(BF16).astype(F32)
    taps = jnp.concatenate([value_taps[:, pl.ds(pl.multiple_of(s * cols, cols), cols)], state_taps[h]], axis=1)
    stage[block] = one_block(heads_here, cols, proj[...], step_proj[...], gate, segs[...].T, segs[0:1, :],
                             taps, head_terms[0:1, :], head_terms[1:2, :], pick[...], carry, state)

    @pl.when(block // per_peer != s)
    def _():
        sending(block).start()

    @pl.when(block // per_peer == s)
    def _():
        keeping(block).start()

    @pl.when(block == count - 1)
    def _():
        for index in range(count):
            @pl.when(index // per_peer != s)
            def _():
                sending(index).wait_send()

            @pl.when(index // per_peer == s)
            def _():
                keeping(index).wait()

        for dist in range(1, SEQ_FAST):
            peer = (s + dist) % SEQ_FAST
            for index in range(per_peer):
                there = out.at[pl.ds(index * block_len, block_len), pl.ds(pl.multiple_of(peer * cols, cols), cols)]
                pltpu.make_async_remote_copy(
                    src_ref=there, dst_ref=there, send_sem=send_sem.at[0], recv_sem=recv_sem.at[peer, index],
                    device_id=(peer, h), device_id_type=MESH).wait_recv()


def layer(tok_all, w_gate, proj, step_proj, segs, value_taps, state_taps, head_terms, pick, heads_here, block_len):
    count = tok_all.shape[0] // block_len
    cols = w_gate.shape[1]
    fixed = lambda array: pl.BlockSpec(array.shape, lambda i: (0,) * array.ndim)
    by_rows = lambda array: pl.BlockSpec((block_len, array.shape[1]), lambda i: (i, 0))
    return pl.pallas_call(
        functools.partial(layer_kernel, heads_here),
        grid=(count,),
        out_shape=jax.ShapeDtypeStruct((tok_all.shape[0] // SEQ_FAST, cols * SEQ_FAST), BF16),
        in_specs=[
            by_rows(tok_all), fixed(w_gate), by_rows(proj), by_rows(step_proj),
            pl.BlockSpec((segs.shape[0], block_len), lambda i: (0, i)),
            fixed(value_taps), fixed(state_taps), fixed(head_terms), fixed(pick),
        ],
        out_specs=pl.BlockSpec(memory_space=pl.ANY),
        scratch_shapes=[
            pltpu.VMEM((8, proj.shape[1]), F32),
            pltpu.VMEM(((proj.shape[1] - cols) // 2, cols), F32),
            pltpu.VMEM((count, block_len, cols), BF16),
            pltpu.SemaphoreType.DMA((count,)),
            pltpu.SemaphoreType.DMA((SEQ_FAST, count // SEQ_FAST)),
            pltpu.SemaphoreType.DMA((count // SEQ_FAST,)),
        ],
        compiler_params=pltpu.CompilerParams(
            collective_id=1, has_side_effects=True, vmem_limit_bytes=48 * 1024 * 1024),
        name="layer",
    )(tok_all, w_gate, proj, step_proj, segs, value_taps, state_taps, head_terms, pick)


def prepared(doc_lengths, step_bias, log_rate, total, cols, heads_here):
    s = lax.axis_index("seq")
    starts = jnp.cumsum(doc_lengths) - doc_lengths
    at = jnp.arange(total)[None, :] - jnp.arange(8)[:, None]
    segs = (jnp.sum((starts[:, None, None] <= at[None]).astype(jnp.int32), axis=0) - 1).astype(F32)
    terms = lax.dynamic_slice_in_dim(jnp.stack([step_bias, log_rate]), s * heads_here, heads_here, 1)
    head_terms = jnp.pad(terms, ((0, 0), (0, STEP_ROWS - heads_here)))
    row, col = np.arange(6 * STEP_ROWS)[:, None], np.arange(2 * cols)[None, :]
    pick = (row % STEP_ROWS == (col % cols) // (cols // heads_here)) & (row // (3 * STEP_ROWS) == col // cols)
    return segs, head_terms, jnp.asarray(pick, BF16)


STEP_ROWS = 16


def local_fast(tokens, doc_lengths, value_weight, gate_weight, state_weight, step_weight,
               value_conv, state_conv, step_bias, log_rate):
    total = tokens.shape[0] * SEQ_FAST * HEAD_FAST
    cols = value_weight.shape[1] // SEQ_FAST
    heads_here = step_weight.shape[1] // SEQ_FAST
    step_parts = step_weight.T.reshape(SEQ_FAST, heads_here, -1)
    step_parts = jnp.pad(step_parts, ((0, 0), (0, STEP_ROWS - heads_here), (0, 0)))
    segs, head_terms, pick = prepared(doc_lengths, step_bias, log_rate, total, cols, heads_here)
    tok_all, _, w_gate, _, proj, step_proj = spread(tokens, value_weight, gate_weight, state_weight, step_parts)
    return layer(tok_all.reshape(total, -1), w_gate, proj, step_proj, segs, value_conv, state_conv, head_terms,
                 pick, heads_here, BLOCK)


def solution(mesh):
    fast = mesh.shape["seq"] == SEQ_FAST and mesh.shape["head"] == HEAD_FAST
    return jax.shard_map(
        local_fast if fast else local,
        mesh=mesh,
        in_specs=(
            P(("seq", "head"), None),
            P(),
            P("seq", "head"),
            P("seq", "head"),
            P(None, "seq", None),
            P("seq", "head"),
            P(None, "head"),
            P(),
            P("head"),
            P("head"),
        ),
        out_specs=P("seq", "head"),
        check_vma=False,
    )
```

```python
import functools

import jax
import jax.numpy as jnp
import numpy as np
from jax import lax
from jax.experimental import pallas as pl
from jax.experimental.pallas import tpu as pltpu
from jax.sharding import PartitionSpec as P

HEADS = 128
GROUPS = 8
BLOCK = 256


def passed_along(value, axis, steps):
    count = lax.axis_size(axis)
    leading, last = (max(0, -steps), min(count, count - steps))
    return lax.ppermute(value, axis, [(source, source + steps) for source in range(leading, last)])


def segment_of(positions, starts):
    reached = (starts[None, :] <= positions[:, None]).astype(jnp.int32)
    return jnp.sum(reached, axis=1) - 1


def causal_conv(extended, taps_weight, seg_ext, row_count):
    tap_count = taps_weight.shape[0]
    own_segment = seg_ext[tap_count - 1 :]
    summed = jnp.zeros((row_count, extended.shape[1]), jnp.float32)
    for tap_index in range(tap_count):
        window = extended[tap_index : tap_index + row_count].astype(jnp.float32)
        keep_mask = (seg_ext[tap_index : tap_index + row_count] == own_segment).astype(jnp.float32)[
            :, None
        ]
        summed = summed + taps_weight[tap_index][None, :] * window * keep_mask
    return jax.nn.silu(summed).astype(jnp.bfloat16)


def block_terms(b_rows, c_rows, x_rows, decay_rows, step_rows, segments, seg_before):
    block_len = b_rows.shape[0]
    head_total = decay_rows.shape[0]
    x_heads = x_rows.reshape(block_len, head_total, -1)
    cumulative = jnp.cumsum(decay_rows, axis=1)
    products = jnp.dot(c_rows, b_rows.T, preferred_element_type=jnp.float32)
    local_index = jnp.arange(block_len)
    allowed = (local_index[None, :] <= local_index[:, None]) & (
        segments[None, :] == segments[:, None]
    )
    spread = cumulative[:, :, None] - cumulative[:, None, :]
    decay_mat = jnp.where(allowed[None], jnp.exp(jnp.where(allowed[None], spread, 0.0)), 0.0)
    scores = (products[None] * decay_mat * step_rows[:, None, :]).astype(jnp.bfloat16)
    y_inner = jnp.einsum("hij,jhp->ihp", scores, x_heads, preferred_element_type=jnp.float32)
    ending = cumulative[:, -1]
    trailing = (
        jnp.where((segments == segments[-1])[None, :], jnp.exp(ending[:, None] - cumulative), 0.0)
        * step_rows
    )
    weighted = (trailing.T[:, :, None] * x_heads.astype(jnp.float32)).astype(jnp.bfloat16)
    local_state = jnp.einsum("jn,jhp->hnp", b_rows, weighted, preferred_element_type=jnp.float32)
    factor = jnp.where(segments[-1] == seg_before, jnp.exp(ending), 0.0)
    entry_gain = jnp.where((segments == seg_before)[None, :], jnp.exp(cumulative), 0.0)
    return (y_inner.reshape(block_len, -1), local_state, factor, entry_gain)


def local_pass(state_cols, value_cols, decay_cols, step_cols, seg_rows, seg_before, block_len):
    block_count = state_cols.shape[0] // block_len
    state_dim = state_cols.shape[1] // 2
    head_total = decay_cols.shape[1]
    b_all = state_cols[:, :state_dim].reshape(block_count, block_len, state_dim)
    c_all = state_cols[:, state_dim:].reshape(block_count, block_len, state_dim)
    x_all = value_cols.reshape(block_count, block_len, -1)
    decay_all = decay_cols.reshape(block_count, block_len, head_total).transpose(0, 2, 1)
    step_all = step_cols.reshape(block_count, block_len, head_total).transpose(0, 2, 1)
    seg_all = seg_rows.reshape(block_count, block_len)

    def one_block(block_item):
        return block_terms(*block_item)

    outputs = lax.map(one_block, (b_all, c_all, x_all, decay_all, step_all, seg_all, seg_before))
    return (outputs, c_all)


def prefix_blocks(local_state, factor):

    def chain_step(carry_pair, block_item):
        running, running_gain = carry_pair
        local_term, factor_term = block_item
        return (
            (factor_term[:, None, None] * running + local_term, factor_term * running_gain),
            (running, running_gain),
        )

    initial = (
        jnp.zeros(local_state.shape[1:], jnp.float32),
        jnp.ones((factor.shape[1],), jnp.float32),
    )
    (shard_state, shard_gain), (inside, gain_list) = lax.scan(
        chain_step, initial, (local_state, factor)
    )
    return (shard_state, shard_gain, inside, gain_list)


def finish(y_inner, incoming, entry_gain, c_all, value_cols, gate_cols):
    block_count, block_len, _ = y_inner.shape
    head_total = incoming.shape[1]
    carried = jnp.einsum(
        "cin,chnp->cihp", c_all.astype(jnp.float32), incoming, precision=lax.Precision.HIGHEST
    )
    carried = carried * entry_gain.transpose(0, 2, 1)[:, :, :, None]
    x_heads = value_cols.reshape(block_count, block_len, head_total, -1).astype(jnp.float32)
    summed = y_inner.reshape(block_count, block_len, head_total, -1) + carried + x_heads
    gating = jax.nn.silu(gate_cols.astype(jnp.float32)).reshape(
        block_count, block_len, head_total, -1
    )
    return (summed * gating).reshape(block_count * block_len, -1).astype(jnp.bfloat16)


def local(
    tokens,
    doc_lengths,
    value_weight,
    gate_weight,
    state_weight,
    step_weight,
    value_conv,
    state_conv,
    step_bias,
    log_rate,
):
    tok_dev = tokens.shape[0] * lax.axis_size("head")
    heads_here = step_weight.shape[1]
    tap_count = value_conv.shape[0]
    group_index = lax.axis_index("head") * heads_here // (HEADS // GROUPS)
    state_own = lax.dynamic_index_in_dim(state_weight, group_index, 0, keepdims=False)
    conv_own = lax.dynamic_index_in_dim(state_conv, group_index, 0, keepdims=False)
    gathered = lax.all_gather(tokens, "head", axis=0, tiled=True)
    shard_pieces = (
        lax.all_gather(value_weight, "seq", axis=0, tiled=True),
        lax.all_gather(gate_weight, "seq", axis=0, tiled=True),
        lax.all_gather(state_own, "seq", axis=0, tiled=True),
        lax.all_gather(step_weight, "seq", axis=0, tiled=True),
    )
    projected = tuple(
        (
            jnp.dot(gathered, weight_piece, preferred_element_type=jnp.float32)
            for weight_piece in shard_pieces
        )
    )
    value_proj = projected[0].astype(jnp.bfloat16)
    gate_proj = projected[1].astype(jnp.bfloat16)
    state_proj = projected[2].astype(jnp.bfloat16)
    step_proj = projected[3].astype(jnp.bfloat16)
    value_cols = value_proj.shape[1]
    rim_source = jnp.concatenate(
        [value_proj[-(tap_count - 1) :], state_proj[-(tap_count - 1) :]], axis=1
    )
    rim_rows = passed_along(rim_source, "seq", 1)
    value_ext = jnp.concatenate([rim_rows[:, :value_cols], value_proj], axis=0)
    state_ext = jnp.concatenate([rim_rows[:, value_cols:], state_proj], axis=0)
    starts = jnp.cumsum(doc_lengths) - doc_lengths
    positions = lax.axis_index("seq") * tok_dev + jnp.arange(-(tap_count - 1), tok_dev)
    seg_ext = segment_of(positions, starts)
    value_act = causal_conv(value_ext, value_conv, seg_ext, tok_dev)
    state_act = causal_conv(state_ext, conv_own, seg_ext, tok_dev)
    step_size = jax.nn.softplus(step_proj.astype(jnp.float32) + step_bias[None, :])
    decay_rate = -jnp.exp(log_rate)[None, :] * step_size
    seg_rows = seg_ext[tap_count - 1 :]
    seg_before = seg_ext[tap_count - 2 : tap_count - 2 + tok_dev : BLOCK]
    (y_inner, local_state, factor, entry_gain), c_all = local_pass(
        state_act, value_act, decay_rate, step_size, seg_rows, seg_before, BLOCK
    )
    shard_state, shard_gain, inside, gain_list = prefix_blocks(local_state, factor)

    def relay(step_index, arriving):
        leaving = shard_gain[:, None, None] * arriving + shard_state
        return passed_along(leaving, "seq", 1)

    entering = lax.fori_loop(0, lax.axis_size("seq") - 1, relay, jnp.zeros_like(shard_state))
    incoming = inside + gain_list[:, :, None, None] * entering[None]
    return finish(y_inner, incoming, entry_gain, c_all, value_act, gate_proj)


MESH = pl.DeviceIdType.MESH
SEQ_FAST, HEAD_FAST = 4, 8
F32 = jnp.float32
BF16 = jnp.bfloat16


def spread_kernel(tok, value_w, gate_w, state_w, step_w, tok_all, w_vs, w_gate, step_all, proj, step_proj,
                  tok_send, tok_recv, wt_send, wt_recv, st_send, st_recv, own_sem, vs_here, step_here, fetch_sem):
    s = lax.axis_index("seq")
    h = lax.axis_index("head")
    y, x, c = h // 4, (h // 2) % 2, h % 2
    part = value_w.shape[0]
    cols = value_w.shape[1] // SEQ_FAST

    def head_of(yy, xx, cc):
        return yy * 4 + xx * 2 + cc

    mate, xnb, ynb = head_of(y, x, 1 - c), head_of(y, 1 - x, c), head_of(1 - y, x, c)
    barrier = pltpu.get_barrier_semaphore()
    for dist in range(1, SEQ_FAST):
        pl.semaphore_signal(barrier, inc=1, device_id=((s + dist) % SEQ_FAST, h), device_id_type=MESH)
    for nb in (mate, xnb, ynb):
        pl.semaphore_signal(barrier, inc=1, device_id=(s, nb), device_id_type=MESH)
    pl.semaphore_wait(barrier, SEQ_FAST + 2)

    def send(src, z, hh, to, kind):
        slot = z * HEAD_FAST + hh
        return pltpu.make_async_remote_copy(
            src_ref=src, dst_ref=tok_all.at[slot], send_sem=tok_send.at[kind, slot],
            recv_sem=tok_recv.at[slot], device_id=to, device_id_type=MESH)

    def arrived(z, hh):
        slot = z * HEAD_FAST + hh
        pltpu.make_async_remote_copy(
            src_ref=tok_all.at[slot], dst_ref=tok_all.at[slot], send_sem=tok_send.at[0, slot],
            recv_sem=tok_recv.at[slot], device_id=(s, mate), device_id_type=MESH).wait_recv()

    UP, DOWN, TOX, TOY, TOMATE = range(5)
    own = pltpu.make_async_copy(tok, tok_all.at[s * HEAD_FAST + h], own_sem.at[0])
    own.start()

    def plane(src, z):
        send(src, z, h, (s, xnb), TOX).start()
        send(src, z, h, (s, ynb), TOY).start()
        send(src, z, h, (s, mate), TOMATE).start()

    @pl.when(s < SEQ_FAST - 1)
    def _():
        send(tok, s, h, (s + 1, h), UP).start()

    @pl.when(s > 0)
    def _():
        send(tok, s, h, (s - 1, h), DOWN).start()

    plane(tok, s)

    def weights(dist):
        peer = (s + dist) % SEQ_FAST
        copies = []
        for which, ref in enumerate((value_w, gate_w)):
            src = ref.at[:, pl.ds(pl.multiple_of(peer * cols, cols), cols)]
            dst = (w_vs, w_gate)[which].at[pl.ds(pl.multiple_of(s * part, part), part), pl.ds(0, cols)]
            copies.append((src, dst, which))
        copies.append((step_w.at[peer], step_all.at[:, pl.ds(pl.multiple_of(s * part, part), part)], 2))
        if dist == 0:
            copies.append((state_w.at[h], w_vs.at[pl.ds(pl.multiple_of(s * part, part), part), pl.ds(cols, state_w.shape[2])], 3))
            return [pltpu.make_async_copy(src, dst, own_sem.at[1 + which]) for src, dst, which in copies]
        return [pltpu.make_async_remote_copy(
            src_ref=src, dst_ref=dst, send_sem=wt_send.at[dist, which], recv_sem=wt_recv.at[dist, which],
            device_id=(peer, h), device_id_type=MESH) for src, dst, which in copies]

    own_weights = weights(0)
    for copy in own_weights:
        copy.start()

    def sent(z, hh, kind):
        send(tok_all.at[z * HEAD_FAST + hh], z, hh, (s, mate), kind).wait_send()

    def state_send(src, z, to, way):
        return pltpu.make_async_remote_copy(
            src_ref=src, dst_ref=w_vs.at[pl.ds(pl.multiple_of(z * part, part), part), pl.ds(cols, state_w.shape[2])],
            send_sem=st_send.at[way, z], recv_sem=st_recv.at[z], device_id=to, device_id_type=MESH)

    def state_piece(z):
        return w_vs.at[pl.ds(pl.multiple_of(z * part, part), part), pl.ds(cols, state_w.shape[2])]

    def both_sides(dist, act):
        @pl.when(s - dist >= 0)
        def _():
            act(s - dist, s < SEQ_FAST - 1, s + 1, UP)

        if dist > 0:
            @pl.when(s + dist < SEQ_FAST)
            def _():
                act(s + dist, s > 0, s - 1, DOWN)

    def token_round(z, onward, nxt, way):
        arrived(z, h)
        block = tok_all.at[z * HEAD_FAST + h]

        @pl.when(onward)
        def _():
            send(block, z, h, (nxt, h), way).start()

        plane(block, z)

    def state_round(z, onward, nxt, way):
        state_send(state_piece(z), z, (nxt, h), way).wait_recv()

        @pl.when(onward)
        def _():
            state_send(state_piece(z), z, (nxt, h), way).start()

    def relay(z, hh, to, kind):
        slot = z * HEAD_FAST + hh
        send(tok_all.at[slot], z, hh, to, kind).start()

    def plane_round(z, onward, nxt, way):
        arrived(z, xnb)

        @pl.when(z % 2 == 0)
        def _():
            relay(z, xnb, (s, ynb), TOY)

        relay(z, xnb, (s, mate), TOMATE)
        arrived(z, ynb)

        @pl.when(z % 2 == 1)
        def _():
            relay(z, ynb, (s, xnb), TOX)

        relay(z, ynb, (s, mate), TOMATE)

    def token_left(z, onward, nxt, way):
        @pl.when(onward)
        def _():
            sent(z, h, way)

    both_sides(1, token_round)
    both_sides(0, plane_round)
    both_sides(2, token_round)

    @pl.when(s < SEQ_FAST - 1)
    def _():
        state_send(state_w.at[h], s, (s + 1, h), UP).start()

    @pl.when(s > 0)
    def _():
        state_send(state_w.at[h], s, (s - 1, h), DOWN).start()

    both_sides(1, plane_round)
    both_sides(3, token_round)
    both_sides(1, state_round)
    both_sides(2, token_left)
    peer_weights = [weights(dist) for dist in range(1, SEQ_FAST)]
    for copies in peer_weights:
        copies[0].start()
        copies[2].start()
    both_sides(2, plane_round)
    both_sides(2, state_round)
    both_sides(3, plane_round)
    for copies in peer_weights:
        copies[0].wait_send()
        copies[1].start()
    diag = head_of(1 - y, 1 - x, c)
    for dist in range(SEQ_FAST):
        z = (s + dist) % SEQ_FAST
        arrived(z, diag)
        relay(z, diag, (s, mate), TOMATE)
    for dist in range(SEQ_FAST):
        z = (s + dist) % SEQ_FAST
        for yy, xx in ((y, x), (y, 1 - x), (1 - y, x), (1 - y, 1 - x)):
            arrived(z, head_of(yy, xx, 1 - c))

    both_sides(3, state_round)
    own.wait()
    for copy in own_weights:
        copy.wait()
    for copies in peer_weights:
        copies[0].wait_recv()
        copies[2].wait()
    fetches = [pltpu.make_async_copy(w_vs, vs_here, fetch_sem.at[0]),
               pltpu.make_async_copy(step_all, step_here, fetch_sem.at[1])]
    for copy in fetches:
        copy.start()
    for copy in fetches:
        copy.wait()

    def project(tokens, proj_to, step_to):
        rows = tokens[...].reshape(-1, tokens.shape[2])
        proj_to[...] = fast_dot(rows, vs_here[...]).astype(BF16)
        step_to[...] = fast_dot(rows, step_here[...], ((1,), (1,))).astype(BF16).astype(F32)

    count, rows, width = tok_all.shape
    pltpu.emit_pipeline(
        project, grid=(count // 2,),
        in_specs=[pl.BlockSpec((2, rows, width), lambda i: (i, 0, 0))],
        out_specs=[pl.BlockSpec((2 * rows, proj.shape[1]), lambda i: (i, 0)),
                   pl.BlockSpec((2 * rows, step_proj.shape[1]), lambda i: (i, 0))],
    )(tok_all, proj, step_proj)
    for copies in peer_weights:
        copies[1].wait()

    for z in range(SEQ_FAST):
        @pl.when((z <= s) & (s < SEQ_FAST - 1))
        def _():
            state_send(state_piece(z), z, (s, mate), UP).wait_send()

        @pl.when((z >= s) & (s > 0))
        def _():
            state_send(state_piece(z), z, (s, mate), DOWN).wait_send()

    @pl.when(s < SEQ_FAST - 1)
    def _():
        sent(s, h, UP)

    @pl.when(s > 0)
    def _():
        sent(s, h, DOWN)

    both_sides(1, token_left)
    both_sides(3, token_left)
    for dist in range(SEQ_FAST):
        z = (s + dist) % SEQ_FAST
        sent(z, h, TOX)
        sent(z, h, TOY)
        for hh in (h, xnb, ynb, diag):
            sent(z, hh, TOMATE)

        @pl.when(z % 2 == 0)
        def _():
            sent(z, xnb, TOY)

        @pl.when(z % 2 == 1)
        def _():
            sent(z, ynb, TOX)


def spread(tokens, value_weight, gate_weight, state_weight, step_parts):
    rows, width = tokens.shape
    part, wide = value_weight.shape
    cols = wide // SEQ_FAST
    any_spec = pl.BlockSpec(memory_space=pl.ANY)
    count = SEQ_FAST * HEAD_FAST
    return pl.pallas_call(
        spread_kernel,
        out_shape=(
            jax.ShapeDtypeStruct((count, rows, width), BF16),
            jax.ShapeDtypeStruct((part * SEQ_FAST, cols + state_weight.shape[2]), BF16),
            jax.ShapeDtypeStruct((part * SEQ_FAST, cols), BF16),
            jax.ShapeDtypeStruct((step_parts.shape[1], part * SEQ_FAST), BF16),
            jax.ShapeDtypeStruct((count * rows, cols + state_weight.shape[2]), BF16),
            jax.ShapeDtypeStruct((count * rows, step_parts.shape[1]), F32),
        ),
        in_specs=[any_spec] * 5,
        out_specs=(any_spec,) * 6,
        scratch_shapes=[
            pltpu.SemaphoreType.DMA((5, count)),
            pltpu.SemaphoreType.DMA((count,)),
            pltpu.SemaphoreType.DMA((SEQ_FAST, 3)),
            pltpu.SemaphoreType.DMA((SEQ_FAST, 3)),
            pltpu.SemaphoreType.DMA((2, SEQ_FAST)),
            pltpu.SemaphoreType.DMA((SEQ_FAST,)),
            pltpu.SemaphoreType.DMA((5,)),
            pltpu.VMEM((part * SEQ_FAST, cols + state_weight.shape[2]), BF16),
            pltpu.VMEM((step_parts.shape[1], part * SEQ_FAST), BF16),
            pltpu.SemaphoreType.DMA((2,)),
        ],
        compiler_params=pltpu.CompilerParams(
            collective_id=0, has_side_effects=True, vmem_limit_bytes=60 * 1024 * 1024),
        name="spread",
    )(tokens, value_weight, gate_weight, state_weight, step_parts)


def fast_dot(left, right, dims=((1,), (0,))):
    return lax.dot_general(left, right, (dims, ((), ())), preferred_element_type=F32)


def silu(value):
    return value * lax.logistic(value)


def parts_of(value):
    high = value.astype(BF16)
    rest = value - high.astype(F32)
    mid = rest.astype(BF16)
    return high, mid, (rest - mid.astype(F32)).astype(BF16)


def one_block(heads_here, cols, proj, step_proj, gate, segments, seg_row, taps, bias, rate, pick, carry, state):
    block_len = proj.shape[0]
    half = block_len // 2
    chan = cols // heads_here
    state_dim = (proj.shape[1] - cols) // 2
    tap_count = taps.shape[0]
    conv_in = proj.astype(F32)
    tail = carry[...]
    carry[...] = conv_in[block_len - 8:]
    extended = jnp.concatenate([tail, conv_in], axis=0)
    summed = conv_in * taps[tap_count - 1:tap_count, :]
    own = segments[:, 0:1]
    for back in range(1, tap_count):
        window = extended[8 - back:8 - back + block_len]
        keep = segments[:, back:back + 1] == own
        summed = summed + jnp.where(keep, taps[tap_count - 1 - back:tap_count - back, :] * window, 0.0)
    act = silu(summed).astype(BF16)
    x = act[:, :cols]
    b_rows = act[:, cols:cols + state_dim]
    c_rows = act[:, cols + state_dim:]

    raw = step_proj + bias
    step = jnp.maximum(raw, 0.0) + jnp.log1p(jnp.exp(-jnp.abs(raw)))
    width = step.shape[1]
    decay = -jnp.exp(rate) * step
    row_id = lax.broadcasted_iota(jnp.int32, (block_len, block_len), 0)
    col_id = lax.broadcasted_iota(jnp.int32, (block_len, block_len), 1)
    lower = col_id <= row_id
    sums = fast_dot(lower.astype(F32).astype(BF16), jnp.concatenate(parts_of(decay), axis=1))
    cum = sums[:, :width] + sums[:, width:2 * width] + sums[:, 2 * width:]
    turned = jnp.concatenate([cum, step], axis=1).T
    cum_t, step_t = turned[:width], turned[width:]
    allowed = lower & (seg_row == own)
    products = jnp.where(allowed, fast_dot(c_rows, b_rows, ((1,), (1,))), 0.0)
    head_of_col = lax.broadcasted_iota(jnp.int32, (1, cols), 1) // chan
    xf = x.astype(F32)
    x_parts = [jnp.where(head_of_col == head, xf, 0.0).astype(BF16) for head in range(heads_here)]

    def rows_of(first, rows, upto):
        scores = []
        for head in range(heads_here):
            spread_ij = jnp.minimum(cum[first:first + rows, head:head + 1] - cum_t[head:head + 1, :upto], 0.0)
            scores.append((products[first:first + rows, :upto] * jnp.exp(spread_ij)
                           * step_t[head:head + 1, :upto]).astype(BF16))
        return fast_dot(jnp.concatenate(scores, axis=1), jnp.concatenate([xp[:upto] for xp in x_parts], axis=0))

    inner = jnp.concatenate([rows_of(0, half, half), rows_of(half, half, block_len)], axis=0)

    ending = cum[block_len - 1:block_len, :]
    trailing = jnp.where(own == own[block_len - 1:block_len], jnp.exp(ending - cum), 0.0) * step
    gain = jnp.where(own == segments[0:1, 1:2], jnp.exp(cum), 0.0)
    wide = fast_dot(jnp.concatenate(parts_of(trailing) + parts_of(gain), axis=1), pick)
    weighted = (wide[:, :cols] * xf).astype(BF16)
    gain_cols = wide[:, cols:]
    entering = state[...]
    high, mid, _ = parts_of(entering)
    carried = fast_dot(jnp.concatenate([c_rows, c_rows], axis=1), jnp.concatenate([high, mid], axis=0))
    state[...] = gain_cols[block_len - 1:block_len, :] * entering + fast_dot(b_rows, weighted, ((0,), (0,)))
    total = inner + gain_cols * carried + xf
    return (total * silu(gate)).astype(BF16)


def layer_kernel(heads_here, tok, w_gate, proj, step_proj, segs, value_taps, state_taps, head_terms, pick, out,
                 carry, state, stage, send_sem, recv_sem, own_sem):
    block = pl.program_id(0)
    count = stage.shape[0]
    block_len, cols = stage.shape[1:]
    per_peer = count // SEQ_FAST
    s = lax.axis_index("seq")
    h = lax.axis_index("head")

    def sending(index):
        return pltpu.make_async_remote_copy(
            src_ref=stage.at[index],
            dst_ref=out.at[pl.ds(pl.multiple_of((index % per_peer) * block_len, block_len), block_len),
                           pl.ds(pl.multiple_of(s * cols, cols), cols)],
            send_sem=send_sem.at[index], recv_sem=recv_sem.at[s, index % per_peer],
            device_id=(index // per_peer, h), device_id_type=MESH)

    def keeping(index):
        return pltpu.make_async_copy(
            stage.at[index],
            out.at[pl.ds(pl.multiple_of((index % per_peer) * block_len, block_len), block_len),
                   pl.ds(pl.multiple_of(s * cols, cols), cols)], own_sem.at[index % per_peer])

    @pl.when(block == 0)
    def _():
        barrier = pltpu.get_barrier_semaphore()
        for dist in range(1, SEQ_FAST):
            pl.semaphore_signal(barrier, inc=1, device_id=((s + dist) % SEQ_FAST, h), device_id_type=MESH)
        pl.semaphore_wait(barrier, SEQ_FAST - 1)
        carry[...] = jnp.zeros_like(carry)
        state[...] = jnp.zeros_like(state)

    gate = fast_dot(tok[...], w_gate[...]).astype(BF16).astype(F32)
    taps = jnp.concatenate([value_taps[:, pl.ds(pl.multiple_of(s * cols, cols), cols)], state_taps[h]], axis=1)
    stage[block] = one_block(heads_here, cols, proj[...], step_proj[...], gate, segs[...].T, segs[0:1, :],
                             taps, head_terms[0:1, :], head_terms[1:2, :], pick[...], carry, state)

    @pl.when(block // per_peer != s)
    def _():
        sending(block).start()

    @pl.when(block // per_peer == s)
    def _():
        keeping(block).start()

    @pl.when(block == count - 1)
    def _():
        for index in range(count):
            @pl.when(index // per_peer != s)
            def _():
                sending(index).wait_send()

            @pl.when(index // per_peer == s)
            def _():
                keeping(index).wait()

        for dist in range(1, SEQ_FAST):
            peer = (s + dist) % SEQ_FAST
            for index in range(per_peer):
                there = out.at[pl.ds(index * block_len, block_len), pl.ds(pl.multiple_of(peer * cols, cols), cols)]
                pltpu.make_async_remote_copy(
                    src_ref=there, dst_ref=there, send_sem=send_sem.at[0], recv_sem=recv_sem.at[peer, index],
                    device_id=(peer, h), device_id_type=MESH).wait_recv()


def layer(tok_all, w_gate, proj, step_proj, segs, value_taps, state_taps, head_terms, pick, heads_here, block_len):
    count = tok_all.shape[0] // block_len
    cols = w_gate.shape[1]
    fixed = lambda array: pl.BlockSpec(array.shape, lambda i: (0,) * array.ndim)
    by_rows = lambda array: pl.BlockSpec((block_len, array.shape[1]), lambda i: (i, 0))
    return pl.pallas_call(
        functools.partial(layer_kernel, heads_here),
        grid=(count,),
        out_shape=jax.ShapeDtypeStruct((tok_all.shape[0] // SEQ_FAST, cols * SEQ_FAST), BF16),
        in_specs=[
            by_rows(tok_all), fixed(w_gate), by_rows(proj), by_rows(step_proj),
            pl.BlockSpec((segs.shape[0], block_len), lambda i: (0, i)),
            fixed(value_taps), fixed(state_taps), fixed(head_terms), fixed(pick),
        ],
        out_specs=pl.BlockSpec(memory_space=pl.ANY),
        scratch_shapes=[
            pltpu.VMEM((8, proj.shape[1]), F32),
            pltpu.VMEM(((proj.shape[1] - cols) // 2, cols), F32),
            pltpu.VMEM((count, block_len, cols), BF16),
            pltpu.SemaphoreType.DMA((count,)),
            pltpu.SemaphoreType.DMA((SEQ_FAST, count // SEQ_FAST)),
            pltpu.SemaphoreType.DMA((count // SEQ_FAST,)),
        ],
        compiler_params=pltpu.CompilerParams(
            collective_id=1, has_side_effects=True, vmem_limit_bytes=60 * 1024 * 1024),
        name="layer",
    )(tok_all, w_gate, proj, step_proj, segs, value_taps, state_taps, head_terms, pick)


def prepared(doc_lengths, step_bias, log_rate, total, cols, heads_here):
    s = lax.axis_index("seq")
    starts = jnp.cumsum(doc_lengths) - doc_lengths
    at = jnp.arange(total)[None, :] - jnp.arange(8)[:, None]
    segs = (jnp.sum((starts[:, None, None] <= at[None]).astype(jnp.int32), axis=0) - 1).astype(F32)
    terms = lax.dynamic_slice_in_dim(jnp.stack([step_bias, log_rate]), s * heads_here, heads_here, 1)
    head_terms = jnp.pad(terms, ((0, 0), (0, STEP_ROWS - heads_here)))
    row, col = np.arange(6 * STEP_ROWS)[:, None], np.arange(2 * cols)[None, :]
    pick = (row % STEP_ROWS == (col % cols) // (cols // heads_here)) & (row // (3 * STEP_ROWS) == col // cols)
    return segs, head_terms, jnp.asarray(pick, BF16)


STEP_ROWS = 16


def local_fast(tokens, doc_lengths, value_weight, gate_weight, state_weight, step_weight,
               value_conv, state_conv, step_bias, log_rate):
    total = tokens.shape[0] * SEQ_FAST * HEAD_FAST
    cols = value_weight.shape[1] // SEQ_FAST
    heads_here = step_weight.shape[1] // SEQ_FAST
    step_parts = step_weight.T.reshape(SEQ_FAST, heads_here, -1)
    step_parts = jnp.pad(step_parts, ((0, 0), (0, STEP_ROWS - heads_here), (0, 0)))
    segs, head_terms, pick = prepared(doc_lengths, step_bias, log_rate, total, cols, heads_here)
    tok_all, _, w_gate, _, proj, step_proj = spread(tokens, value_weight, gate_weight, state_weight, step_parts)
    return layer(tok_all.reshape(total, -1), w_gate, proj, step_proj, segs, value_conv, state_conv, head_terms,
                 pick, heads_here, BLOCK)


def solution(mesh):
    fast = mesh.shape["seq"] == SEQ_FAST and mesh.shape["head"] == HEAD_FAST
    return jax.shard_map(
        local_fast if fast else local,
        mesh=mesh,
        in_specs=(
            P(("seq", "head"), None),
            P(),
            P("seq", "head"),
            P("seq", "head"),
            P(None, "seq", None),
            P("seq", "head"),
            P(None, "head"),
            P(),
            P("head"),
            P("head"),
        ),
        out_specs=P("seq", "head"),
        check_vma=False,
    )
```

```python
import functools

import jax
import jax.numpy as jnp
import numpy as np
from jax import lax
from jax.experimental import pallas as pl
from jax.experimental.pallas import tpu as pltpu
from jax.sharding import PartitionSpec as P

HEADS = 128
GROUPS = 8
BLOCK = 256


def passed_along(value, axis, steps):
    count = lax.axis_size(axis)
    leading, last = (max(0, -steps), min(count, count - steps))
    return lax.ppermute(value, axis, [(source, source + steps) for source in range(leading, last)])


def segment_of(positions, starts):
    reached = (starts[None, :] <= positions[:, None]).astype(jnp.int32)
    return jnp.sum(reached, axis=1) - 1


def causal_conv(extended, taps_weight, seg_ext, row_count):
    tap_count = taps_weight.shape[0]
    own_segment = seg_ext[tap_count - 1 :]
    summed = jnp.zeros((row_count, extended.shape[1]), jnp.float32)
    for tap_index in range(tap_count):
        window = extended[tap_index : tap_index + row_count].astype(jnp.float32)
        keep_mask = (seg_ext[tap_index : tap_index + row_count] == own_segment).astype(jnp.float32)[
            :, None
        ]
        summed = summed + taps_weight[tap_index][None, :] * window * keep_mask
    return jax.nn.silu(summed).astype(jnp.bfloat16)


def block_terms(b_rows, c_rows, x_rows, decay_rows, step_rows, segments, seg_before):
    block_len = b_rows.shape[0]
    head_total = decay_rows.shape[0]
    x_heads = x_rows.reshape(block_len, head_total, -1)
    cumulative = jnp.cumsum(decay_rows, axis=1)
    products = jnp.dot(c_rows, b_rows.T, preferred_element_type=jnp.float32)
    local_index = jnp.arange(block_len)
    allowed = (local_index[None, :] <= local_index[:, None]) & (
        segments[None, :] == segments[:, None]
    )
    spread = cumulative[:, :, None] - cumulative[:, None, :]
    decay_mat = jnp.where(allowed[None], jnp.exp(jnp.where(allowed[None], spread, 0.0)), 0.0)
    scores = (products[None] * decay_mat * step_rows[:, None, :]).astype(jnp.bfloat16)
    y_inner = jnp.einsum("hij,jhp->ihp", scores, x_heads, preferred_element_type=jnp.float32)
    ending = cumulative[:, -1]
    trailing = (
        jnp.where((segments == segments[-1])[None, :], jnp.exp(ending[:, None] - cumulative), 0.0)
        * step_rows
    )
    weighted = (trailing.T[:, :, None] * x_heads.astype(jnp.float32)).astype(jnp.bfloat16)
    local_state = jnp.einsum("jn,jhp->hnp", b_rows, weighted, preferred_element_type=jnp.float32)
    factor = jnp.where(segments[-1] == seg_before, jnp.exp(ending), 0.0)
    entry_gain = jnp.where((segments == seg_before)[None, :], jnp.exp(cumulative), 0.0)
    return (y_inner.reshape(block_len, -1), local_state, factor, entry_gain)


def local_pass(state_cols, value_cols, decay_cols, step_cols, seg_rows, seg_before, block_len):
    block_count = state_cols.shape[0] // block_len
    state_dim = state_cols.shape[1] // 2
    head_total = decay_cols.shape[1]
    b_all = state_cols[:, :state_dim].reshape(block_count, block_len, state_dim)
    c_all = state_cols[:, state_dim:].reshape(block_count, block_len, state_dim)
    x_all = value_cols.reshape(block_count, block_len, -1)
    decay_all = decay_cols.reshape(block_count, block_len, head_total).transpose(0, 2, 1)
    step_all = step_cols.reshape(block_count, block_len, head_total).transpose(0, 2, 1)
    seg_all = seg_rows.reshape(block_count, block_len)

    def one_block(block_item):
        return block_terms(*block_item)

    outputs = lax.map(one_block, (b_all, c_all, x_all, decay_all, step_all, seg_all, seg_before))
    return (outputs, c_all)


def prefix_blocks(local_state, factor):

    def chain_step(carry_pair, block_item):
        running, running_gain = carry_pair
        local_term, factor_term = block_item
        return (
            (factor_term[:, None, None] * running + local_term, factor_term * running_gain),
            (running, running_gain),
        )

    initial = (
        jnp.zeros(local_state.shape[1:], jnp.float32),
        jnp.ones((factor.shape[1],), jnp.float32),
    )
    (shard_state, shard_gain), (inside, gain_list) = lax.scan(
        chain_step, initial, (local_state, factor)
    )
    return (shard_state, shard_gain, inside, gain_list)


def finish(y_inner, incoming, entry_gain, c_all, value_cols, gate_cols):
    block_count, block_len, _ = y_inner.shape
    head_total = incoming.shape[1]
    carried = jnp.einsum(
        "cin,chnp->cihp", c_all.astype(jnp.float32), incoming, precision=lax.Precision.HIGHEST
    )
    carried = carried * entry_gain.transpose(0, 2, 1)[:, :, :, None]
    x_heads = value_cols.reshape(block_count, block_len, head_total, -1).astype(jnp.float32)
    summed = y_inner.reshape(block_count, block_len, head_total, -1) + carried + x_heads
    gating = jax.nn.silu(gate_cols.astype(jnp.float32)).reshape(
        block_count, block_len, head_total, -1
    )
    return (summed * gating).reshape(block_count * block_len, -1).astype(jnp.bfloat16)


def local(
    tokens,
    doc_lengths,
    value_weight,
    gate_weight,
    state_weight,
    step_weight,
    value_conv,
    state_conv,
    step_bias,
    log_rate,
):
    tok_dev = tokens.shape[0] * lax.axis_size("head")
    heads_here = step_weight.shape[1]
    tap_count = value_conv.shape[0]
    group_index = lax.axis_index("head") * heads_here // (HEADS // GROUPS)
    state_own = lax.dynamic_index_in_dim(state_weight, group_index, 0, keepdims=False)
    conv_own = lax.dynamic_index_in_dim(state_conv, group_index, 0, keepdims=False)
    gathered = lax.all_gather(tokens, "head", axis=0, tiled=True)
    shard_pieces = (
        lax.all_gather(value_weight, "seq", axis=0, tiled=True),
        lax.all_gather(gate_weight, "seq", axis=0, tiled=True),
        lax.all_gather(state_own, "seq", axis=0, tiled=True),
        lax.all_gather(step_weight, "seq", axis=0, tiled=True),
    )
    projected = tuple(
        (
            jnp.dot(gathered, weight_piece, preferred_element_type=jnp.float32)
            for weight_piece in shard_pieces
        )
    )
    value_proj = projected[0].astype(jnp.bfloat16)
    gate_proj = projected[1].astype(jnp.bfloat16)
    state_proj = projected[2].astype(jnp.bfloat16)
    step_proj = projected[3].astype(jnp.bfloat16)
    value_cols = value_proj.shape[1]
    rim_source = jnp.concatenate(
        [value_proj[-(tap_count - 1) :], state_proj[-(tap_count - 1) :]], axis=1
    )
    rim_rows = passed_along(rim_source, "seq", 1)
    value_ext = jnp.concatenate([rim_rows[:, :value_cols], value_proj], axis=0)
    state_ext = jnp.concatenate([rim_rows[:, value_cols:], state_proj], axis=0)
    starts = jnp.cumsum(doc_lengths) - doc_lengths
    positions = lax.axis_index("seq") * tok_dev + jnp.arange(-(tap_count - 1), tok_dev)
    seg_ext = segment_of(positions, starts)
    value_act = causal_conv(value_ext, value_conv, seg_ext, tok_dev)
    state_act = causal_conv(state_ext, conv_own, seg_ext, tok_dev)
    step_size = jax.nn.softplus(step_proj.astype(jnp.float32) + step_bias[None, :])
    decay_rate = -jnp.exp(log_rate)[None, :] * step_size
    seg_rows = seg_ext[tap_count - 1 :]
    seg_before = seg_ext[tap_count - 2 : tap_count - 2 + tok_dev : BLOCK]
    (y_inner, local_state, factor, entry_gain), c_all = local_pass(
        state_act, value_act, decay_rate, step_size, seg_rows, seg_before, BLOCK
    )
    shard_state, shard_gain, inside, gain_list = prefix_blocks(local_state, factor)

    def relay(step_index, arriving):
        leaving = shard_gain[:, None, None] * arriving + shard_state
        return passed_along(leaving, "seq", 1)

    entering = lax.fori_loop(0, lax.axis_size("seq") - 1, relay, jnp.zeros_like(shard_state))
    incoming = inside + gain_list[:, :, None, None] * entering[None]
    return finish(y_inner, incoming, entry_gain, c_all, value_act, gate_proj)


MESH = pl.DeviceIdType.MESH
SEQ_FAST, HEAD_FAST = 4, 8
F32 = jnp.float32
BF16 = jnp.bfloat16


def spread_kernel(tok, value_w, gate_w, state_w, step_w, tok_all, w_vs, w_gate, step_all, proj, step_proj,
                  tok_send, tok_recv, wt_send, wt_recv, st_send, st_recv, own_sem, vs_here, step_here, fetch_sem):
    s = lax.axis_index("seq")
    h = lax.axis_index("head")
    y, x, c = h // 4, (h // 2) % 2, h % 2
    part = value_w.shape[0]
    cols = value_w.shape[1] // SEQ_FAST

    def head_of(yy, xx, cc):
        return yy * 4 + xx * 2 + cc

    mate, xnb, ynb = head_of(y, x, 1 - c), head_of(y, 1 - x, c), head_of(1 - y, x, c)
    barrier = pltpu.get_barrier_semaphore()
    for dist in range(1, SEQ_FAST):
        pl.semaphore_signal(barrier, inc=1, device_id=((s + dist) % SEQ_FAST, h), device_id_type=MESH)
    for nb in (mate, xnb, ynb):
        pl.semaphore_signal(barrier, inc=1, device_id=(s, nb), device_id_type=MESH)
    pl.semaphore_wait(barrier, SEQ_FAST + 2)

    def send(src, z, hh, to, kind):
        slot = z * HEAD_FAST + hh
        return pltpu.make_async_remote_copy(
            src_ref=src, dst_ref=tok_all.at[slot], send_sem=tok_send.at[kind, slot],
            recv_sem=tok_recv.at[slot], device_id=to, device_id_type=MESH)

    def arrived(z, hh):
        slot = z * HEAD_FAST + hh
        pltpu.make_async_remote_copy(
            src_ref=tok_all.at[slot], dst_ref=tok_all.at[slot], send_sem=tok_send.at[0, slot],
            recv_sem=tok_recv.at[slot], device_id=(s, mate), device_id_type=MESH).wait_recv()

    UP, DOWN, TOX, TOY, TOMATE = range(5)
    own = pltpu.make_async_copy(tok, tok_all.at[s * HEAD_FAST + h], own_sem.at[0])
    own.start()

    def plane(src, z):
        send(src, z, h, (s, xnb), TOX).start()
        send(src, z, h, (s, ynb), TOY).start()
        send(src, z, h, (s, mate), TOMATE).start()

    @pl.when(s < SEQ_FAST - 1)
    def _():
        send(tok, s, h, (s + 1, h), UP).start()

    @pl.when(s > 0)
    def _():
        send(tok, s, h, (s - 1, h), DOWN).start()

    plane(tok, s)

    def weights(dist):
        peer = (s + dist) % SEQ_FAST
        copies = []
        for which, ref in enumerate((value_w, gate_w)):
            src = ref.at[:, pl.ds(pl.multiple_of(peer * cols, cols), cols)]
            dst = (w_vs, w_gate)[which].at[pl.ds(pl.multiple_of(s * part, part), part), pl.ds(0, cols)]
            copies.append((src, dst, which))
        copies.append((step_w.at[peer], step_all.at[:, pl.ds(pl.multiple_of(s * part, part), part)], 2))
        if dist == 0:
            copies.append((state_w.at[h], w_vs.at[pl.ds(pl.multiple_of(s * part, part), part), pl.ds(cols, state_w.shape[2])], 3))
            return [pltpu.make_async_copy(src, dst, own_sem.at[1 + which]) for src, dst, which in copies]
        return [pltpu.make_async_remote_copy(
            src_ref=src, dst_ref=dst, send_sem=wt_send.at[dist, which], recv_sem=wt_recv.at[dist, which],
            device_id=(peer, h), device_id_type=MESH) for src, dst, which in copies]

    own_weights = weights(0)
    for copy in own_weights:
        copy.start()

    def sent(z, hh, kind):
        send(tok_all.at[z * HEAD_FAST + hh], z, hh, (s, mate), kind).wait_send()

    def state_send(src, z, to, way):
        return pltpu.make_async_remote_copy(
            src_ref=src, dst_ref=w_vs.at[pl.ds(pl.multiple_of(z * part, part), part), pl.ds(cols, state_w.shape[2])],
            send_sem=st_send.at[way, z], recv_sem=st_recv.at[z], device_id=to, device_id_type=MESH)

    def state_piece(z):
        return w_vs.at[pl.ds(pl.multiple_of(z * part, part), part), pl.ds(cols, state_w.shape[2])]

    def both_sides(dist, act):
        @pl.when(s - dist >= 0)
        def _():
            act(s - dist, s < SEQ_FAST - 1, s + 1, UP)

        if dist > 0:
            @pl.when(s + dist < SEQ_FAST)
            def _():
                act(s + dist, s > 0, s - 1, DOWN)

    def token_round(z, onward, nxt, way):
        arrived(z, h)
        block = tok_all.at[z * HEAD_FAST + h]

        @pl.when(onward)
        def _():
            send(block, z, h, (nxt, h), way).start()

        plane(block, z)

    def state_round(z, onward, nxt, way):
        state_send(state_piece(z), z, (nxt, h), way).wait_recv()

        @pl.when(onward)
        def _():
            state_send(state_piece(z), z, (nxt, h), way).start()

    def relay(z, hh, to, kind):
        slot = z * HEAD_FAST + hh
        send(tok_all.at[slot], z, hh, to, kind).start()

    def plane_round(z, onward, nxt, way):
        arrived(z, xnb)

        @pl.when(z % 2 == 0)
        def _():
            relay(z, xnb, (s, ynb), TOY)

        relay(z, xnb, (s, mate), TOMATE)
        arrived(z, ynb)

        @pl.when(z % 2 == 1)
        def _():
            relay(z, ynb, (s, xnb), TOX)

        relay(z, ynb, (s, mate), TOMATE)

    def token_left(z, onward, nxt, way):
        @pl.when(onward)
        def _():
            sent(z, h, way)

    both_sides(1, token_round)
    both_sides(0, plane_round)
    both_sides(2, token_round)

    @pl.when(s < SEQ_FAST - 1)
    def _():
        state_send(state_w.at[h], s, (s + 1, h), UP).start()

    @pl.when(s > 0)
    def _():
        state_send(state_w.at[h], s, (s - 1, h), DOWN).start()

    both_sides(1, plane_round)
    both_sides(3, token_round)
    both_sides(1, state_round)
    both_sides(2, token_left)
    peer_weights = [weights(dist) for dist in range(1, SEQ_FAST)]
    for copies in peer_weights:
        copies[0].start()
        copies[2].start()
    both_sides(2, plane_round)
    both_sides(2, state_round)
    both_sides(3, plane_round)
    for copies in peer_weights:
        copies[0].wait_send()
        copies[1].start()
    diag = head_of(1 - y, 1 - x, c)
    for dist in range(SEQ_FAST):
        z = (s + dist) % SEQ_FAST
        arrived(z, diag)
        relay(z, diag, (s, mate), TOMATE)
    for dist in range(SEQ_FAST):
        z = (s + dist) % SEQ_FAST
        for yy, xx in ((y, x), (y, 1 - x), (1 - y, x), (1 - y, 1 - x)):
            arrived(z, head_of(yy, xx, 1 - c))

    both_sides(3, state_round)
    own.wait()
    for copy in own_weights:
        copy.wait()
    for copies in peer_weights:
        copies[0].wait_recv()
        copies[2].wait()
    fetches = [pltpu.make_async_copy(w_vs, vs_here, fetch_sem.at[0]),
               pltpu.make_async_copy(step_all, step_here, fetch_sem.at[1])]
    for copy in fetches:
        copy.start()
    for copy in fetches:
        copy.wait()

    def project(tokens, proj_to, step_to):
        rows = tokens[...].reshape(-1, tokens.shape[2])
        proj_to[...] = fast_dot(rows, vs_here[...]).astype(BF16)
        step_to[...] = fast_dot(rows, step_here[...], ((1,), (1,))).astype(BF16).astype(F32)

    count, rows, width = tok_all.shape
    pltpu.emit_pipeline(
        project, grid=(count // 4,),
        in_specs=[pl.BlockSpec((4, rows, width), lambda i: (i, 0, 0))],
        out_specs=[pl.BlockSpec((4 * rows, proj.shape[1]), lambda i: (i, 0)),
                   pl.BlockSpec((4 * rows, step_proj.shape[1]), lambda i: (i, 0))],
    )(tok_all, proj, step_proj)
    for copies in peer_weights:
        copies[1].wait()

    for z in range(SEQ_FAST):
        @pl.when((z <= s) & (s < SEQ_FAST - 1))
        def _():
            state_send(state_piece(z), z, (s, mate), UP).wait_send()

        @pl.when((z >= s) & (s > 0))
        def _():
            state_send(state_piece(z), z, (s, mate), DOWN).wait_send()

    @pl.when(s < SEQ_FAST - 1)
    def _():
        sent(s, h, UP)

    @pl.when(s > 0)
    def _():
        sent(s, h, DOWN)

    both_sides(1, token_left)
    both_sides(3, token_left)
    for dist in range(SEQ_FAST):
        z = (s + dist) % SEQ_FAST
        sent(z, h, TOX)
        sent(z, h, TOY)
        for hh in (h, xnb, ynb, diag):
            sent(z, hh, TOMATE)

        @pl.when(z % 2 == 0)
        def _():
            sent(z, xnb, TOY)

        @pl.when(z % 2 == 1)
        def _():
            sent(z, ynb, TOX)


def spread(tokens, value_weight, gate_weight, state_weight, step_parts):
    rows, width = tokens.shape
    part, wide = value_weight.shape
    cols = wide // SEQ_FAST
    any_spec = pl.BlockSpec(memory_space=pl.ANY)
    count = SEQ_FAST * HEAD_FAST
    return pl.pallas_call(
        spread_kernel,
        out_shape=(
            jax.ShapeDtypeStruct((count, rows, width), BF16),
            jax.ShapeDtypeStruct((part * SEQ_FAST, cols + state_weight.shape[2]), BF16),
            jax.ShapeDtypeStruct((part * SEQ_FAST, cols), BF16),
            jax.ShapeDtypeStruct((step_parts.shape[1], part * SEQ_FAST), BF16),
            jax.ShapeDtypeStruct((count * rows, cols + state_weight.shape[2]), BF16),
            jax.ShapeDtypeStruct((count * rows, step_parts.shape[1]), F32),
        ),
        in_specs=[any_spec] * 5,
        out_specs=(any_spec,) * 6,
        scratch_shapes=[
            pltpu.SemaphoreType.DMA((5, count)),
            pltpu.SemaphoreType.DMA((count,)),
            pltpu.SemaphoreType.DMA((SEQ_FAST, 3)),
            pltpu.SemaphoreType.DMA((SEQ_FAST, 3)),
            pltpu.SemaphoreType.DMA((2, SEQ_FAST)),
            pltpu.SemaphoreType.DMA((SEQ_FAST,)),
            pltpu.SemaphoreType.DMA((5,)),
            pltpu.VMEM((part * SEQ_FAST, cols + state_weight.shape[2]), BF16),
            pltpu.VMEM((step_parts.shape[1], part * SEQ_FAST), BF16),
            pltpu.SemaphoreType.DMA((2,)),
        ],
        compiler_params=pltpu.CompilerParams(
            collective_id=0, has_side_effects=True, vmem_limit_bytes=60 * 1024 * 1024),
        name="spread",
    )(tokens, value_weight, gate_weight, state_weight, step_parts)


def fast_dot(left, right, dims=((1,), (0,))):
    return lax.dot_general(left, right, (dims, ((), ())), preferred_element_type=F32)


def silu(value):
    return value * lax.logistic(value)


def parts_of(value):
    high = value.astype(BF16)
    rest = value - high.astype(F32)
    mid = rest.astype(BF16)
    return high, mid, (rest - mid.astype(F32)).astype(BF16)


def one_block(heads_here, cols, proj, step_proj, gate, segments, seg_row, taps, bias, rate, pick, carry, state):
    block_len = proj.shape[0]
    half = block_len // 2
    chan = cols // heads_here
    state_dim = (proj.shape[1] - cols) // 2
    tap_count = taps.shape[0]
    conv_in = proj.astype(F32)
    tail = carry[...]
    carry[...] = conv_in[block_len - 8:]
    extended = jnp.concatenate([tail, conv_in], axis=0)
    summed = conv_in * taps[tap_count - 1:tap_count, :]
    own = segments[:, 0:1]
    for back in range(1, tap_count):
        window = extended[8 - back:8 - back + block_len]
        keep = segments[:, back:back + 1] == own
        summed = summed + jnp.where(keep, taps[tap_count - 1 - back:tap_count - back, :] * window, 0.0)
    act = silu(summed).astype(BF16)
    x = act[:, :cols]
    b_rows = act[:, cols:cols + state_dim]
    c_rows = act[:, cols + state_dim:]

    raw = step_proj + bias
    step = jnp.maximum(raw, 0.0) + jnp.log1p(jnp.exp(-jnp.abs(raw)))
    width = step.shape[1]
    decay = -jnp.exp(rate) * step
    row_id = lax.broadcasted_iota(jnp.int32, (block_len, block_len), 0)
    col_id = lax.broadcasted_iota(jnp.int32, (block_len, block_len), 1)
    lower = col_id <= row_id
    sums = fast_dot(lower.astype(F32).astype(BF16), jnp.concatenate(parts_of(decay), axis=1))
    cum = sums[:, :width] + sums[:, width:2 * width] + sums[:, 2 * width:]
    turned = jnp.concatenate([cum, step], axis=1).T
    cum_t, step_t = turned[:width], turned[width:]
    allowed = lower & (seg_row == own)
    products = jnp.where(allowed, fast_dot(c_rows, b_rows, ((1,), (1,))), 0.0)
    head_of_col = lax.broadcasted_iota(jnp.int32, (1, cols), 1) // chan
    xf = x.astype(F32)
    x_parts = [jnp.where(head_of_col == head, xf, 0.0).astype(BF16) for head in range(heads_here)]

    def rows_of(first, rows, upto):
        scores = []
        for head in range(heads_here):
            spread_ij = jnp.minimum(cum[first:first + rows, head:head + 1] - cum_t[head:head + 1, :upto], 0.0)
            scores.append((products[first:first + rows, :upto] * jnp.exp(spread_ij)
                           * step_t[head:head + 1, :upto]).astype(BF16))
        return fast_dot(jnp.concatenate(scores, axis=1), jnp.concatenate([xp[:upto] for xp in x_parts], axis=0))

    inner = jnp.concatenate([rows_of(0, half, half), rows_of(half, half, block_len)], axis=0)

    ending = cum[block_len - 1:block_len, :]
    trailing = jnp.where(own == own[block_len - 1:block_len], jnp.exp(ending - cum), 0.0) * step
    gain = jnp.where(own == segments[0:1, 1:2], jnp.exp(cum), 0.0)
    wide = fast_dot(jnp.concatenate(parts_of(trailing) + parts_of(gain), axis=1), pick)
    weighted = (wide[:, :cols] * xf).astype(BF16)
    gain_cols = wide[:, cols:]
    entering = state[...]
    high, mid, _ = parts_of(entering)
    carried = fast_dot(jnp.concatenate([c_rows, c_rows], axis=1), jnp.concatenate([high, mid], axis=0))
    state[...] = gain_cols[block_len - 1:block_len, :] * entering + fast_dot(b_rows, weighted, ((0,), (0,)))
    total = inner + gain_cols * carried + xf
    return (total * silu(gate)).astype(BF16)


def layer_kernel(heads_here, tok, w_gate, proj, step_proj, segs, value_taps, state_taps, head_terms, pick, out,
                 carry, state, stage, send_sem, recv_sem, own_sem):
    step_id = pl.program_id(0)
    count = stage.shape[0]
    block_len, cols = stage.shape[1:]
    per_peer = count // SEQ_FAST
    s = lax.axis_index("seq")
    h = lax.axis_index("head")

    def sending(index):
        return pltpu.make_async_remote_copy(
            src_ref=stage.at[index],
            dst_ref=out.at[pl.ds(pl.multiple_of((index % per_peer) * block_len, block_len), block_len),
                           pl.ds(pl.multiple_of(s * cols, cols), cols)],
            send_sem=send_sem.at[index], recv_sem=recv_sem.at[s, index % per_peer],
            device_id=(index // per_peer, h), device_id_type=MESH)

    def keeping(index):
        return pltpu.make_async_copy(
            stage.at[index],
            out.at[pl.ds(pl.multiple_of((index % per_peer) * block_len, block_len), block_len),
                   pl.ds(pl.multiple_of(s * cols, cols), cols)], own_sem.at[index % per_peer])

    @pl.when(step_id == 0)
    def _():
        barrier = pltpu.get_barrier_semaphore()
        for dist in range(1, SEQ_FAST):
            pl.semaphore_signal(barrier, inc=1, device_id=((s + dist) % SEQ_FAST, h), device_id_type=MESH)
        pl.semaphore_wait(barrier, SEQ_FAST - 1)
        carry[...] = jnp.zeros_like(carry)
        state[...] = jnp.zeros_like(state)

    gate = fast_dot(tok[...], w_gate[...]).astype(BF16).astype(F32)
    taps = jnp.concatenate([value_taps[:, pl.ds(pl.multiple_of(s * cols, cols), cols)], state_taps[h]], axis=1)
    across = segs[...]
    down = across.T
    for sub in range(PAIR):
        low, high = sub * block_len, (sub + 1) * block_len
        stage[step_id * PAIR + sub] = one_block(
            heads_here, cols, proj[low:high, :], step_proj[low:high, :], gate[low:high], down[low:high],
            across[0:1, low:high], taps, head_terms[0:1, :], head_terms[1:2, :], pick[...], carry, state)

    for sub in range(PAIR):
        block = step_id * PAIR + sub

        @pl.when(block // per_peer != s)
        def _():
            sending(block).start()

        @pl.when(block // per_peer == s)
        def _():
            keeping(block).start()

    @pl.when(step_id == pl.num_programs(0) - 1)
    def _():
        for index in range(count):
            @pl.when(index // per_peer != s)
            def _():
                sending(index).wait_send()

            @pl.when(index // per_peer == s)
            def _():
                keeping(index).wait()

        for dist in range(1, SEQ_FAST):
            peer = (s + dist) % SEQ_FAST
            for index in range(per_peer):
                there = out.at[pl.ds(index * block_len, block_len), pl.ds(pl.multiple_of(peer * cols, cols), cols)]
                pltpu.make_async_remote_copy(
                    src_ref=there, dst_ref=there, send_sem=send_sem.at[0], recv_sem=recv_sem.at[peer, index],
                    device_id=(peer, h), device_id_type=MESH).wait_recv()


def layer(tok_all, w_gate, proj, step_proj, segs, value_taps, state_taps, head_terms, pick, heads_here, block_len):
    count = tok_all.shape[0] // block_len
    cols = w_gate.shape[1]
    fixed = lambda array: pl.BlockSpec(array.shape, lambda i: (0,) * array.ndim)
    by_rows = lambda array: pl.BlockSpec((PAIR * block_len, array.shape[1]), lambda i: (i, 0))
    return pl.pallas_call(
        functools.partial(layer_kernel, heads_here),
        grid=(count // PAIR,),
        out_shape=jax.ShapeDtypeStruct((tok_all.shape[0] // SEQ_FAST, cols * SEQ_FAST), BF16),
        in_specs=[
            by_rows(tok_all), fixed(w_gate), by_rows(proj), by_rows(step_proj),
            pl.BlockSpec((segs.shape[0], PAIR * block_len), lambda i: (0, i)),
            fixed(value_taps), fixed(state_taps), fixed(head_terms), fixed(pick),
        ],
        out_specs=pl.BlockSpec(memory_space=pl.ANY),
        scratch_shapes=[
            pltpu.VMEM((8, proj.shape[1]), F32),
            pltpu.VMEM(((proj.shape[1] - cols) // 2, cols), F32),
            pltpu.VMEM((count, block_len, cols), BF16),
            pltpu.SemaphoreType.DMA((count,)),
            pltpu.SemaphoreType.DMA((SEQ_FAST, count // SEQ_FAST)),
            pltpu.SemaphoreType.DMA((count // SEQ_FAST,)),
        ],
        compiler_params=pltpu.CompilerParams(
            collective_id=1, has_side_effects=True, vmem_limit_bytes=60 * 1024 * 1024),
        name="layer",
    )(tok_all, w_gate, proj, step_proj, segs, value_taps, state_taps, head_terms, pick)


def prepared(doc_lengths, step_bias, log_rate, total, cols, heads_here):
    s = lax.axis_index("seq")
    starts = jnp.cumsum(doc_lengths) - doc_lengths
    at = jnp.arange(total)[None, :] - jnp.arange(8)[:, None]
    segs = (jnp.sum((starts[:, None, None] <= at[None]).astype(jnp.int32), axis=0) - 1).astype(F32)
    terms = lax.dynamic_slice_in_dim(jnp.stack([step_bias, log_rate]), s * heads_here, heads_here, 1)
    head_terms = jnp.pad(terms, ((0, 0), (0, STEP_ROWS - heads_here)))
    row, col = np.arange(6 * STEP_ROWS)[:, None], np.arange(2 * cols)[None, :]
    pick = (row % STEP_ROWS == (col % cols) // (cols // heads_here)) & (row // (3 * STEP_ROWS) == col // cols)
    return segs, head_terms, jnp.asarray(pick, BF16)


STEP_ROWS = 16
PAIR = 2


def local_fast(tokens, doc_lengths, value_weight, gate_weight, state_weight, step_weight,
               value_conv, state_conv, step_bias, log_rate):
    total = tokens.shape[0] * SEQ_FAST * HEAD_FAST
    cols = value_weight.shape[1] // SEQ_FAST
    heads_here = step_weight.shape[1] // SEQ_FAST
    step_parts = step_weight.T.reshape(SEQ_FAST, heads_here, -1)
    step_parts = jnp.pad(step_parts, ((0, 0), (0, STEP_ROWS - heads_here), (0, 0)))
    segs, head_terms, pick = prepared(doc_lengths, step_bias, log_rate, total, cols, heads_here)
    tok_all, _, w_gate, _, proj, step_proj = spread(tokens, value_weight, gate_weight, state_weight, step_parts)
    return layer(tok_all.reshape(total, -1), w_gate, proj, step_proj, segs, value_conv, state_conv, head_terms,
                 pick, heads_here, BLOCK)


def solution(mesh):
    fast = mesh.shape["seq"] == SEQ_FAST and mesh.shape["head"] == HEAD_FAST
    return jax.shard_map(
        local_fast if fast else local,
        mesh=mesh,
        in_specs=(
            P(("seq", "head"), None),
            P(),
            P("seq", "head"),
            P("seq", "head"),
            P(None, "seq", None),
            P("seq", "head"),
            P(None, "head"),
            P(),
            P("head"),
            P("head"),
        ),
        out_specs=P("seq", "head"),
        check_vma=False,
    )
```
